32 devices in a mesh: grp: 4 (over x, core), seq: 8 (over z, y).
Axes of the slice: x: 2, y: 2, z: 4, core: 2. Of those that a mesh axis runs over, the one named last changes fastest.
Arguments:
- queries: bfloat16 [4096, 3072], P(('grp', 'seq')), may hold values from -6 to 6, as said below
- key_states: bfloat16 [4096, 3072], P(('grp', 'seq')), may hold values from -6 to 6
- value_states: bfloat16 [4096, 3072], P(('grp', 'seq')), may hold values from -16 to 16
- key_keep: int32 [4096], P(('grp', 'seq')), may hold values 0 or 1
- summary_pos: int32 [4], replicated, may hold values from 0 to 7
Outputs:
- attended: bfloat16 [4096, 3072], P(('grp', 'seq'))
The draws below stay inside these ranges and needn't reach their ends.
Inputs may be any that keep to these rules, and one draw needn't show every extreme that they name: queries and key_states entries lie within -6 to 6.
All inputs are finite; a program needn't handle non-finite values. No bound on the sum of `key_keep` on one device may be relied on, other than what follows from the above.
Results may differ from the reference program's by a relative error of at most 0.008.
Values may be sent and summed in bfloat16 or wider, within the bound.
A program may use at most 64 MiB of HBM per device.

```python
import math
import jax
import jax.numpy as jnp
from jax import lax

HEADS = 24
HEAD_DIM = 128
FIXED_HEADS = 4
LOCAL_HEADS = 16
BLOCK = 128
LOOKBACK = 2
STRIDE = 8
WINDOWS = 4
BLOCKS = 32
TOKENS = 4096


def draw_pair(key):
    full_shape = (TOKENS, HEADS * HEAD_DIM)
    query_base = jnp.clip(jax.random.normal(jax.random.fold_in(key, 1), full_shape, jnp.float32), -6.0, 6.0)
    key_base = jnp.clip(1.5 * jax.random.normal(jax.random.fold_in(key, 2), full_shape, jnp.float32), -6.0, 6.0)
    return (query_base, key_base)


def draw_queries(key, part):
    return draw_pair(key)[0].astype(jnp.bfloat16)


def draw_key_states(key, part):
    return draw_pair(key)[1].astype(jnp.bfloat16)


def place_ends(result, stream_key, smallest, high):
    longest = result.shape.index(max(result.shape))
    spots = []
    for shift in (0, 1):
        where = [jax.random.randint(jax.random.fold_in(stream_key, axis), (), 0, length) for axis, length in enumerate(result.shape)]
        where[longest] = (where[longest] + shift) % result.shape[longest]
        spots.append(tuple(where))
    return result.at[spots[0]].set(smallest).at[spots[1]].set(high)


def block_scale(rng, dims, cuts, low, largest):
    def one(dim, blocks):
        steps = jax.random.uniform(jax.random.fold_in(jax.random.fold_in(rng, 6), dim), (blocks,), jnp.float32, low / len(cuts), largest / len(cuts))
        return jnp.repeat(jnp.exp(steps), dims[dim] // blocks).reshape((-1,) + (1,) * (len(dims) - dim - 1))

    loudness = one(*cuts[0])
    for cut in cuts[1:]:
        loudness = loudness * one(*cut)
    return loudness


def centred(stream_key, shape, scale, most, pieces=(), held_as=jnp.bfloat16):
    level = block_scale(stream_key, shape, pieces, -0.22, 0.18) if pieces else 1.0
    values = jax.random.normal(stream_key, shape, jnp.float32) * scale * level
    return jnp.minimum(jnp.maximum(values, -most), most).astype(held_as)


def setup_inputs(seed: int = 0) -> dict:
    keys = jax.random.split(jax.random.key(seed), 6)
    return {
        "queries": draw_queries(jax.random.fold_in(keys[5], 71), 0),
        "key_states": draw_key_states(jax.random.fold_in(keys[5], 71), 0),
        "value_states": centred(keys[2], (TOKENS, HEADS * HEAD_DIM), 4.0, 16.0, ((0, 32),)),
        "key_keep": place_ends((jax.random.randint(keys[3], (TOKENS,), 0, 8) < 7).astype(jnp.int32), jax.random.fold_in(keys[3], 1), 0, 1),
        "summary_pos": place_ends(jax.random.randint(keys[4], (WINDOWS,), 0, STRIDE), jax.random.fold_in(keys[4], 1), 0, STRIDE - 1).astype(jnp.int32),
    }


NEG = -1e+30

def softmax_attend(query_heads, key_heads, value_heads, allowed):
    scores = jnp.einsum('hqd,hkd->hqk', query_heads, key_heads) / math.sqrt(HEAD_DIM)
    scores = jnp.where(allowed[None], scores, NEG)
    row_max = lax.optimization_barrier(jnp.max(scores, axis=2, keepdims=True))
    weights = jnp.where(allowed[None], jnp.exp(scores - row_max), 0.0)
    row_sum = lax.optimization_barrier(jnp.sum(weights, axis=2, keepdims=True))
    rounded = lax.optimization_barrier(weights.astype(jnp.bfloat16)).astype(jnp.float32)
    weighted = jnp.einsum('hqk,hkd->hqd', rounded, value_heads)
    return weighted / row_sum

def heads_first(block_rows):
    return jnp.transpose(block_rows.astype(jnp.float32), (1, 0, 2))

def reference(queries, key_states, value_states, key_keep, summary_pos):
    query_blocks = queries.reshape(BLOCKS, BLOCK, HEADS, HEAD_DIM)
    key_blocks = key_states.reshape(BLOCKS, BLOCK, HEADS, HEAD_DIM)
    value_blocks = value_states.reshape(BLOCKS, BLOCK, HEADS, HEAD_DIM)
    keep_blocks = key_keep.reshape(BLOCKS, BLOCK)
    windows = jnp.arange(WINDOWS, dtype=jnp.int32)
    lane_ids = jnp.arange(BLOCK, dtype=jnp.int32)
    fixed_lo = LOCAL_HEADS
    fixed_hi = LOCAL_HEADS + FIXED_HEADS

    def one_block(block_id):
        window = block_id // STRIDE
        column = block_id % STRIDE
        query_pos = block_id * BLOCK + lane_ids
        near_ids = block_id - LOOKBACK + jnp.arange(LOOKBACK + 1, dtype=jnp.int32)
        near_valid = near_ids >= 0
        near_safe = jnp.maximum(near_ids, 0).astype(jnp.int32)
        key_pos = (near_safe[:, None] * BLOCK + lane_ids[None, :]).reshape(-1)
        near_keep = keep_blocks[near_safe].reshape(-1) == 1
        valid_rep = jnp.repeat(near_valid, BLOCK)
        diagonal = key_pos[None, :] == query_pos[:, None]
        near_allowed = valid_rep[None, :] & (key_pos[None, :] <= query_pos[:, None]) & (near_keep[None, :] | diagonal)
        query_heads = heads_first(query_blocks[block_id])
        key_heads = heads_first(key_blocks[near_safe].reshape(-1, HEADS, HEAD_DIM))
        value_heads = heads_first(value_blocks[near_safe].reshape(-1, HEADS, HEAD_DIM))

        def far_part(blocks, valid, head_lo, head_hi):
            far_keys = key_blocks[blocks][:, :, head_lo:head_hi].reshape(-1, head_hi - head_lo, HEAD_DIM)
            far_values = value_blocks[blocks][:, :, head_lo:head_hi].reshape(-1, head_hi - head_lo, HEAD_DIM)
            far_keep = keep_blocks[blocks].reshape(-1) == 1
            far_valid = jnp.repeat(valid, BLOCK) & far_keep
            allowed = jnp.concatenate([near_allowed, jnp.broadcast_to(far_valid[None, :], (BLOCK, far_valid.shape[0]))], axis=1)
            all_keys = jnp.concatenate([key_heads[head_lo:head_hi], heads_first(far_keys)], axis=1)
            all_values = jnp.concatenate([value_heads[head_lo:head_hi], heads_first(far_values)], axis=1)
            return softmax_attend(query_heads[head_lo:head_hi], all_keys, all_values, allowed)
        fixed_blocks = (windows * STRIDE + summary_pos).astype(jnp.int32)
        fixed_valid = fixed_blocks < block_id - LOOKBACK
        strided_blocks = (windows * STRIDE + column).astype(jnp.int32)
        strided_valid = windows < window
        local_out = softmax_attend(query_heads[:fixed_lo], key_heads[:fixed_lo], value_heads[:fixed_lo], near_allowed)
        fixed_out = far_part(fixed_blocks, fixed_valid, fixed_lo, fixed_hi)
        strided_out = far_part(strided_blocks, strided_valid, fixed_hi, HEADS)
        weighted = jnp.concatenate([local_out, fixed_out, strided_out], axis=0)
        return jnp.transpose(weighted, (1, 0, 2)).reshape(BLOCK, HEADS * HEAD_DIM).astype(jnp.bfloat16)
    attended = lax.map(one_block, jnp.arange(BLOCKS, dtype=jnp.int32))
    return attended.reshape(TOKENS, HEADS * HEAD_DIM)
```

```python
import functools
import math

import jax
import jax.numpy as jnp
from jax import lax
from jax.experimental import pallas as pl
from jax.experimental.pallas import tpu as pltpu
from jax.sharding import PartitionSpec as P

HEADS = 24
HEAD_DIM = 128
FIXED_HEADS = 4
STRIDED_HEADS = 4
LOCAL_HEADS = 16
BLOCK = 128
LOOKBACK = 2
WIDTH = HEADS * HEAD_DIM

CHUNK_HEADS = 4
CHUNK = CHUNK_HEADS * HEAD_DIM
CHUNKS = HEADS // CHUNK_HEADS
FIXED_CHUNK = LOCAL_HEADS // CHUNK_HEADS
STRIDED_CHUNK = (LOCAL_HEADS + FIXED_HEADS) // CHUNK_HEADS
ORDER = tuple(range(FIXED_CHUNK)) + (STRIDED_CHUNK, FIXED_CHUNK)
FAR_ROWS = BLOCK + 16
FAR_COLS = 2 * CHUNK

NEG = -1e30
SCALE = math.log2(math.e) / math.sqrt(HEAD_DIM)
MESH = pl.DeviceIdType.MESH


def kernel(
    stride, groups, pos_ref, q_ref, k_ref, v_ref, keep_ref, o_ref,
    kcat, vcat, keeps, bias, st_src, st_buf, cur, rcv, fx_buf,
    halo_send, halo_recv, keep_send, keep_recv, ch_send, ch_recv,
    st_send, st_recv, fx_send, fx_recv,
):
    steps = stride.bit_length() - 1
    blocks = stride * groups
    window = lax.axis_index("grp")
    column = lax.axis_index("seq")
    me = window * stride + column
    odd = lax.rem(column, 2)
    is_odd = odd == 1
    is_even = odd == 0

    def device(block):
        return (lax.div(block, stride), lax.rem(block, stride))

    def partner(step):
        bit = 1 << step
        mine = lax.rem(lax.div(column, bit), 2)
        return (window, column + bit * (1 - 2 * mine))

    def cols(chunk):
        return pl.ds(chunk * CHUNK, CHUNK)

    barrier = pltpu.get_barrier_semaphore()
    greeted = 0
    for away in (-2, -1, 1, 2):
        there = (me + away >= 0) & (me + away < blocks)

        @pl.when(there)
        def _():
            pl.semaphore_signal(barrier, inc=1, device_id=device(me + away), device_id_type=MESH)

        greeted = greeted + there.astype(jnp.int32)
    for step in range(steps):
        pl.semaphore_signal(barrier, inc=1, device_id=partner(step), device_id_type=MESH)
    for away in range(1, groups):
        other = lax.rem(window + away, groups)
        pl.semaphore_signal(barrier, inc=1, device_id=(other, column), device_id_type=MESH)

    keep_row = keep_ref[...].astype(jnp.float32)
    keep_tile = jnp.broadcast_to(keep_row, (16, BLOCK)).astype(jnp.bfloat16)
    keeps[2] = keep_tile
    for buf, chunk in ((st_src, STRIDED_CHUNK), (cur.at[0], FIXED_CHUNK)):
        buf[0:BLOCK, 0:CHUNK] = k_ref[:, cols(chunk)]
        buf[0:BLOCK, CHUNK:FAR_COLS] = v_ref[:, cols(chunk)]
        for lane in range(0, FAR_COLS, BLOCK):
            buf[BLOCK:FAR_ROWS, lane : lane + BLOCK] = keep_tile

    pl.semaphore_wait(barrier, greeted + (steps + groups - 1))

    def keep_copy(ahead):
        slot = LOOKBACK - ahead
        return pltpu.make_async_remote_copy(
            src_ref=keeps.at[2], dst_ref=keeps.at[slot],
            send_sem=keep_send.at[slot], recv_sem=keep_recv.at[slot],
            device_id=device(jnp.minimum(me + ahead, blocks - 1)), device_id_type=MESH)

    def chain_copy(step):
        return pltpu.make_async_remote_copy(
            src_ref=cur.at[step], dst_ref=rcv.at[step],
            send_sem=ch_send.at[step], recv_sem=ch_recv.at[step],
            device_id=partner(step), device_id_type=MESH)

    def group_copy(src, buf, send_sem, recv_sem, away):
        return pltpu.make_async_remote_copy(
            src_ref=src, dst_ref=buf.at[window],
            send_sem=send_sem.at[away - 1], recv_sem=recv_sem.at[window],
            device_id=(window + away, column), device_id_type=MESH)

    def group_arrival(src, buf, send_sem, recv_sem, slot):
        return pltpu.make_async_remote_copy(
            src_ref=src, dst_ref=buf.at[slot],
            send_sem=send_sem.at[0], recv_sem=recv_sem.at[slot],
            device_id=(slot, column), device_id_type=MESH)

    def halo_copy(slot, part, chunk, src, target):
        cat = (kcat, vcat)[part]
        return pltpu.make_async_remote_copy(
            src_ref=src, dst_ref=cat.at[pl.ds(slot * BLOCK, BLOCK), cols(chunk)],
            send_sem=halo_send.at[slot, part, chunk], recv_sem=halo_recv.at[slot, part, chunk],
            device_id=device(target), device_id_type=MESH)

    def own(part, chunk):
        return (k_ref, v_ref)[part].at[:, cols(chunk)]

    def ahead_two(part, chunk):
        return halo_copy(0, part, chunk, own(part, chunk), me + 2)

    def ahead_one(part, chunk):
        return halo_copy(1, part, chunk, own(part, chunk), me + 1)

    def forward(part, chunk):
        src = (kcat, vcat)[part].at[pl.ds(0, BLOCK), cols(chunk)]
        return halo_copy(1, part, chunk, src, me - 1)

    has_two_ahead = me + 2 < blocks
    has_one_ahead = me + 1 < blocks
    has_two_back = me >= 2
    has_one_back = me >= 1
    forwards = is_odd & has_two_back

    @pl.when(has_one_ahead)
    def _():
        keep_copy(1).start()

    @pl.when(has_two_ahead)
    def _():
        keep_copy(2).start()

    chain_copy(0).start()
    for away in range(1, groups):

        @pl.when(window + away < groups)
        def _():
            group_copy(st_src, st_buf, st_send, st_recv, away).start()

    for chunk in ORDER:

        @pl.when(has_two_ahead)
        def _():
            for part in (0, 1):
                ahead_two(part, chunk).start()

        @pl.when(is_even)
        def _():
            for part in (0, 1):
                ahead_one(part, chunk).start()

    kcat[2 * BLOCK : 3 * BLOCK, :] = k_ref[...]
    vcat[2 * BLOCK : 3 * BLOCK, :] = v_ref[...]

    @pl.when(me < 2)
    def _():
        keeps[0] = jnp.zeros((16, BLOCK), jnp.bfloat16)
        kcat[0:BLOCK, :] = jnp.zeros((BLOCK, WIDTH), jnp.bfloat16)
        vcat[0:BLOCK, :] = jnp.zeros((BLOCK, WIDTH), jnp.bfloat16)

    @pl.when(me < 1)
    def _():
        keeps[1] = jnp.zeros((16, BLOCK), jnp.bfloat16)
        kcat[BLOCK : 2 * BLOCK, :] = jnp.zeros((BLOCK, WIDTH), jnp.bfloat16)
        vcat[BLOCK : 2 * BLOCK, :] = jnp.zeros((BLOCK, WIDTH), jnp.bfloat16)

    for slot in range(groups - 1):

        @pl.when(slot >= window)
        def _():
            st_buf[slot] = jnp.zeros((FAR_ROWS, FAR_COLS), jnp.bfloat16)
            fx_buf[slot] = jnp.zeros((FAR_ROWS, FAR_COLS), jnp.bfloat16)

    @pl.when(has_two_back)
    def _():
        keep_copy(2).wait_recv()

    @pl.when(has_one_back)
    def _():
        keep_copy(1).wait_recv()

    def as_bias(flags):
        return jnp.where(flags > 0.5, 0.0, NEG)

    for slot in (0, 1):
        row = as_bias(keeps[slot][0:1, :].astype(jnp.float32))
        bias[:, slot * BLOCK : (slot + 1) * BLOCK] = jnp.broadcast_to(row, (BLOCK, BLOCK))
    query_ids = lax.broadcasted_iota(jnp.int32, (BLOCK, BLOCK), 0)
    key_ids = lax.broadcasted_iota(jnp.int32, (BLOCK, BLOCK), 1)
    flags = jnp.where(key_ids == query_ids, 1.0, jnp.broadcast_to(keep_row, (BLOCK, BLOCK)))
    bias[:, 2 * BLOCK :] = as_bias(jnp.where(key_ids <= query_ids, flags, 0.0))

    def attend(chunk, far):
        rows = []
        for buf, flag in far:
            keep = buf[BLOCK : BLOCK + 16, 0:BLOCK].astype(jnp.float32)[0:1, :]
            rows.append(as_bias(keep * flag))
        for h in range(CHUNK_HEADS):
            at = chunk * CHUNK + h * HEAD_DIM
            head = pl.ds(at, HEAD_DIM)
            q = q_ref[:, head]
            nt = (((1,), (1,)), ((), ()))
            near = lax.dot_general(q, kcat[:, head], nt, preferred_element_type=jnp.float32)
            scores = [near * SCALE + bias[...]]
            for (buf, _), row in zip(far, rows):
                keys = buf[0:BLOCK, h * HEAD_DIM : (h + 1) * HEAD_DIM]
                term = lax.dot_general(q, keys, nt, preferred_element_type=jnp.float32)
                scores.append(term * SCALE + row)
            top = jnp.max(scores[0], axis=1, keepdims=True)
            for s in scores[1:]:
                top = jnp.maximum(top, jnp.max(s, axis=1, keepdims=True))
            total = 0.0
            weighted = 0.0
            for i, s in enumerate(scores):
                w = jnp.exp2(s - top)
                total = total + jnp.sum(w, axis=1, keepdims=True)
                if i == 0:
                    values = vcat[:, head]
                else:
                    values = far[i - 1][0][0:BLOCK, CHUNK + h * HEAD_DIM : CHUNK + (h + 1) * HEAD_DIM]
                weighted = weighted + jnp.dot(
                    w.astype(jnp.bfloat16), values, preferred_element_type=jnp.float32)
            o_ref[:, head] = (weighted / total).astype(jnp.bfloat16)

    def chain_step(step):
        chain_copy(step).wait_recv()
        bit = 1 << step
        theirs = lax.rem(lax.div(pos_ref[window], bit), 2)
        mine = lax.rem(lax.div(column, bit), 2)
        take = jnp.abs(theirs - mine).astype(jnp.float32)
        kept = cur[step].astype(jnp.float32) * (1.0 - take) + rcv[step].astype(jnp.float32) * take
        cur[step + 1] = kept.astype(jnp.bfloat16)
        if step + 1 < steps:
            chain_copy(step + 1).start()
        else:
            for away in range(1, groups):

                @pl.when(window + away < groups)
                def _():
                    group_copy(cur.at[steps], fx_buf, fx_send, fx_recv, away).start()

    for turn, chunk in enumerate(ORDER):
        if turn < steps:
            chain_step(turn)

        @pl.when(has_two_back)
        def _():
            for part in (0, 1):
                ahead_two(part, chunk).wait_recv()

        @pl.when(forwards)
        def _():
            for part in (0, 1):
                forward(part, chunk).start()

        @pl.when(has_one_back)
        def _():
            for part in (0, 1):
                ahead_one(part, chunk).wait_recv()

        far = []
        if chunk == STRIDED_CHUNK:
            for slot in range(groups - 1):

                @pl.when(slot < window)
                def _():
                    group_arrival(st_src, st_buf, st_send, st_recv, slot).wait_recv()

                far.append((st_buf.at[slot], (slot < window).astype(jnp.float32)))
        if chunk == FIXED_CHUNK:
            for slot in range(groups - 1):

                @pl.when(slot < window)
                def _():
                    group_arrival(st_src, fx_buf, fx_send, fx_recv, slot).wait_recv()

                used = (slot < window) & (slot * stride + pos_ref[slot] < me - LOOKBACK)
                far.append((fx_buf.at[slot], used.astype(jnp.float32)))
            used = window * stride + pos_ref[window] < me - LOOKBACK
            far.append((cur.at[steps], used.astype(jnp.float32)))
        attend(chunk, far)

    @pl.when(has_one_ahead)
    def _():
        keep_copy(1).wait_send()

    @pl.when(has_two_ahead)
    def _():
        keep_copy(2).wait_send()
        for chunk in ORDER:
            for part in (0, 1):
                ahead_two(part, chunk).wait_send()

    @pl.when(is_even | forwards)
    def _():
        for chunk in ORDER:
            for part in (0, 1):
                ahead_one(part, chunk).wait_send()

    for step in range(steps):
        chain_copy(step).wait_send()
    for away in range(1, groups):

        @pl.when(window + away < groups)
        def _():
            group_copy(st_src, st_buf, st_send, st_recv, away).wait_send()
            group_copy(cur.at[steps], fx_buf, fx_send, fx_recv, away).wait_send()


def on_device(queries, key_states, value_states, key_keep, summary_pos, *, stride, groups):
    steps = stride.bit_length() - 1
    assert 1 << steps == stride and steps < CHUNKS
    vmem = pl.BlockSpec(memory_space=pltpu.VMEM)
    dma = pltpu.SemaphoreType.DMA
    far = (FAR_ROWS, FAR_COLS)
    return pl.pallas_call(
        functools.partial(kernel, stride, groups),
        out_shape=jax.ShapeDtypeStruct((BLOCK, WIDTH), jnp.bfloat16),
        in_specs=[pl.BlockSpec(memory_space=pltpu.SMEM), vmem, vmem, vmem, vmem],
        out_specs=vmem,
        scratch_shapes=[
            pltpu.VMEM((3 * BLOCK, WIDTH), jnp.bfloat16),
            pltpu.VMEM((3 * BLOCK, WIDTH), jnp.bfloat16),
            pltpu.VMEM((3, 16, BLOCK), jnp.bfloat16),
            pltpu.VMEM((BLOCK, 3 * BLOCK), jnp.float32),
            pltpu.VMEM(far, jnp.bfloat16),
            pltpu.VMEM((groups - 1,) + far, jnp.bfloat16),
            pltpu.VMEM((steps + 1,) + far, jnp.bfloat16),
            pltpu.VMEM((steps,) + far, jnp.bfloat16),
            pltpu.VMEM((groups - 1,) + far, jnp.bfloat16),
            dma((2, 2, CHUNKS)), dma((2, 2, CHUNKS)),
            dma((2,)), dma((2,)),
            dma((steps,)), dma((steps,)),
            dma((groups - 1,)), dma((groups - 1,)),
            dma((groups - 1,)), dma((groups - 1,)),
        ],
        compiler_params=pltpu.CompilerParams(
            collective_id=0, has_side_effects=True, vmem_limit_bytes=40 * 1024 * 1024),
    )(summary_pos, queries, key_states, value_states, key_keep.reshape(1, BLOCK))


def solution(mesh):
    rows = P(("grp", "seq"), None)
    return jax.shard_map(
        functools.partial(on_device, stride=mesh.shape["seq"], groups=mesh.shape["grp"]),
        mesh=mesh,
        in_specs=(rows, rows, rows, P(("grp", "seq")), P()),
        out_specs=rows,
        check_vma=False,
    )
```

```python
import functools
import math

import jax
import jax.numpy as jnp
from jax import lax
from jax.experimental import pallas as pl
from jax.experimental.pallas import tpu as pltpu
from jax.sharding import PartitionSpec as P

HEADS = 24
HEAD_DIM = 128
FIXED_HEADS = 4
STRIDED_HEADS = 4
LOCAL_HEADS = 16
BLOCK = 128
LOOKBACK = 2
WIDTH = HEADS * HEAD_DIM

CHUNK_HEADS = 4
CHUNK = CHUNK_HEADS * HEAD_DIM
CHUNKS = HEADS // CHUNK_HEADS
FIXED_CHUNK = LOCAL_HEADS // CHUNK_HEADS
STRIDED_CHUNK = (LOCAL_HEADS + FIXED_HEADS) // CHUNK_HEADS
ORDER = tuple(range(FIXED_CHUNK)) + (STRIDED_CHUNK, FIXED_CHUNK)
FAR_ROWS = BLOCK + 16
FAR_COLS = 2 * CHUNK

AHEAD = 2
NEG = -1e30
SCALE = math.log2(math.e) / math.sqrt(HEAD_DIM)
MESH = pl.DeviceIdType.MESH


def kernel(
    stride, groups, pos_ref, q_hbm, k_hbm, v_hbm, keep_ref, o_ref,
    q_ref, kcat, vcat, keeps, bias, st_src, st_buf, cur, rcv, fx_buf,
    halo_send, halo_recv, keep_send, keep_recv, ch_send, ch_recv,
    st_send, st_recv, st_pass, fx_send, fx_recv, fx_pass, load_sem,
):
    steps = stride.bit_length() - 1
    blocks = stride * groups
    window = lax.axis_index("grp")
    column = lax.axis_index("seq")
    me = window * stride + column
    odd = lax.rem(column, 2)
    is_odd = odd == 1
    is_even = odd == 0
    core = lax.rem(window, 2)
    chip = window - core
    own_rows = pl.ds(LOOKBACK * BLOCK, BLOCK)
    loads = [
        pltpu.make_async_copy(src, dst, load_sem.at[i])
        for i, (src, dst) in enumerate(
            ((k_hbm, kcat.at[own_rows]), (v_hbm, vcat.at[own_rows]), (q_hbm, q_ref)))
    ]
    for load in loads:
        load.start()

    def device(block):
        return (lax.div(block, stride), lax.rem(block, stride))

    def partner(step):
        bit = 1 << step
        mine = lax.rem(lax.div(column, bit), 2)
        return (window, column + bit * (1 - 2 * mine))

    def cols(chunk):
        return pl.ds(chunk * CHUNK, CHUNK)

    barrier = pltpu.get_barrier_semaphore()
    greeted = 0
    for away in (-2, -1, 1, 2):
        there = (me + away >= 0) & (me + away < blocks)

        @pl.when(there)
        def _():
            pl.semaphore_signal(barrier, inc=1, device_id=device(me + away), device_id_type=MESH)

        greeted = greeted + there.astype(jnp.int32)
    for step in range(steps):
        pl.semaphore_signal(barrier, inc=1, device_id=partner(step), device_id_type=MESH)
    for away in range(1, groups):
        other = lax.rem(window + away, groups)
        pl.semaphore_signal(barrier, inc=1, device_id=(other, column), device_id_type=MESH)

    keep_row = keep_ref[...].astype(jnp.float32)
    keep_tile = jnp.broadcast_to(keep_row, (16, BLOCK)).astype(jnp.bfloat16)
    keeps[2] = keep_tile
    loads[0].wait()
    loads[1].wait()
    for buf, chunk in ((st_src, STRIDED_CHUNK), (cur.at[0], FIXED_CHUNK)):
        buf[0:BLOCK, 0:CHUNK] = kcat[own_rows, cols(chunk)]
        buf[0:BLOCK, CHUNK:FAR_COLS] = vcat[own_rows, cols(chunk)]
        for lane in range(0, FAR_COLS, BLOCK):
            buf[BLOCK:FAR_ROWS, lane : lane + BLOCK] = keep_tile

    pl.semaphore_wait(barrier, greeted + (steps + groups - 1))

    def keep_copy(ahead):
        slot = LOOKBACK - ahead
        return pltpu.make_async_remote_copy(
            src_ref=keeps.at[2], dst_ref=keeps.at[slot],
            send_sem=keep_send.at[slot], recv_sem=keep_recv.at[slot],
            device_id=device(jnp.minimum(me + ahead, blocks - 1)), device_id_type=MESH)

    def chain_copy(step):
        return pltpu.make_async_remote_copy(
            src_ref=cur.at[step], dst_ref=rcv.at[step],
            send_sem=ch_send.at[step], recv_sem=ch_recv.at[step],
            device_id=partner(step), device_id_type=MESH)

    def group_copy(src, buf, send_sem, recv_sem, away):
        return pltpu.make_async_remote_copy(
            src_ref=src, dst_ref=buf.at[window],
            send_sem=send_sem.at[away - 1], recv_sem=recv_sem.at[window],
            device_id=(window + away, column), device_id_type=MESH)

    def halo_copy(slot, part, chunk, src, target):
        cat = (kcat, vcat)[part]
        return pltpu.make_async_remote_copy(
            src_ref=src, dst_ref=cat.at[pl.ds(slot * BLOCK, BLOCK), cols(chunk)],
            send_sem=halo_send.at[slot, part, chunk], recv_sem=halo_recv.at[slot, part, chunk],
            device_id=device(target), device_id_type=MESH)

    def own(part, chunk):
        return (kcat, vcat)[part].at[own_rows, cols(chunk)]

    def ahead_two(part, chunk):
        return halo_copy(0, part, chunk, own(part, chunk), me + 2)

    def ahead_one(part, chunk):
        return halo_copy(1, part, chunk, own(part, chunk), me + 1)

    def forward(part, chunk):
        src = (kcat, vcat)[part].at[pl.ds(0, BLOCK), cols(chunk)]
        return halo_copy(1, part, chunk, src, me - 1)

    has_two_ahead = me + 2 < blocks
    has_one_ahead = me + 1 < blocks
    has_two_back = me >= 2
    has_one_back = me >= 1
    forwards = is_odd & has_two_back

    @pl.when(has_one_ahead)
    def _():
        keep_copy(1).start()

    @pl.when(has_two_ahead)
    def _():
        keep_copy(2).start()

    def goes(away):
        if away == 1:
            return core == 0
        return (window + away < groups) & (away % 2 == 0)

    def send_groups(src, buf, send_sem, recv_sem, act):
        for away in range(1, groups):
            if away == 1 or away % 2 == 0:

                @pl.when(goes(away))
                def _():
                    act(group_copy(src, buf, send_sem, recv_sem, away))

    def pass_copy(buf, recv_sem, pass_sem, slot):
        return pltpu.make_async_remote_copy(
            src_ref=buf.at[slot], dst_ref=buf.at[slot],
            send_sem=pass_sem.at[slot], recv_sem=recv_sem.at[slot],
            device_id=(chip + 1 - core, column), device_id_type=MESH)

    def passes(slot):
        return (slot < chip) & (core == slot % 2)

    def pass_groups(buf, recv_sem, pass_sem):
        for slot in range(groups - 2):

            @pl.when(passes(slot))
            def _():
                copy = pass_copy(buf, recv_sem, pass_sem, slot)
                copy.wait_recv()
                copy.start()

    def rest_of_groups(buf, recv_sem, pass_sem):
        for slot in range(groups - 1):

            @pl.when((slot < window) & jnp.logical_not(passes(slot)))
            def _():
                pass_copy(buf, recv_sem, pass_sem, slot).wait_recv()

    def passed_on(buf, recv_sem, pass_sem):
        for slot in range(groups - 2):

            @pl.when(passes(slot))
            def _():
                pass_copy(buf, recv_sem, pass_sem, slot).wait_send()

    chain_copy(0).start()
    send_groups(st_src, st_buf, st_send, st_recv, lambda copy: copy.start())

    def send_chunk(chunk):

        @pl.when(has_two_ahead)
        def _():
            for part in (0, 1):
                ahead_two(part, chunk).start()

        @pl.when(is_even)
        def _():
            for part in (0, 1):
                ahead_one(part, chunk).start()

    for chunk in ORDER[:AHEAD]:
        send_chunk(chunk)

    @pl.when(me < 2)
    def _():
        keeps[0] = jnp.zeros((16, BLOCK), jnp.bfloat16)
        kcat[0:BLOCK, :] = jnp.zeros((BLOCK, WIDTH), jnp.bfloat16)
        vcat[0:BLOCK, :] = jnp.zeros((BLOCK, WIDTH), jnp.bfloat16)

    @pl.when(me < 1)
    def _():
        keeps[1] = jnp.zeros((16, BLOCK), jnp.bfloat16)
        kcat[BLOCK : 2 * BLOCK, :] = jnp.zeros((BLOCK, WIDTH), jnp.bfloat16)
        vcat[BLOCK : 2 * BLOCK, :] = jnp.zeros((BLOCK, WIDTH), jnp.bfloat16)

    for slot in range(groups - 1):

        @pl.when(slot >= window)
        def _():
            st_buf[slot] = jnp.zeros((FAR_ROWS, FAR_COLS), jnp.bfloat16)
            fx_buf[slot] = jnp.zeros((FAR_ROWS, FAR_COLS), jnp.bfloat16)

    @pl.when(has_two_back)
    def _():
        keep_copy(2).wait_recv()

    @pl.when(has_one_back)
    def _():
        keep_copy(1).wait_recv()

    def as_bias(flags):
        return jnp.where(flags > 0.5, 0.0, NEG)

    for slot in (0, 1):
        row = as_bias(keeps[slot][0:1, :].astype(jnp.float32))
        bias[:, slot * BLOCK : (slot + 1) * BLOCK] = jnp.broadcast_to(row, (BLOCK, BLOCK))
    query_ids = lax.broadcasted_iota(jnp.int32, (BLOCK, BLOCK), 0)
    key_ids = lax.broadcasted_iota(jnp.int32, (BLOCK, BLOCK), 1)
    flags = jnp.where(key_ids == query_ids, 1.0, jnp.broadcast_to(keep_row, (BLOCK, BLOCK)))
    bias[:, 2 * BLOCK :] = as_bias(jnp.where(key_ids <= query_ids, flags, 0.0))

    def attend(chunk, far):
        rows = []
        for buf, flag in far:
            keep = buf[BLOCK : BLOCK + 16, 0:BLOCK].astype(jnp.float32)[0:1, :]
            rows.append(as_bias(keep * flag))
        for h in range(CHUNK_HEADS):
            at = chunk * CHUNK + h * HEAD_DIM
            head = pl.ds(at, HEAD_DIM)
            q = q_ref[:, head]
            nt = (((1,), (1,)), ((), ()))
            near = lax.dot_general(q, kcat[:, head], nt, preferred_element_type=jnp.float32)
            scores = [near * SCALE + bias[...]]
            for (buf, _), row in zip(far, rows):
                keys = buf[0:BLOCK, h * HEAD_DIM : (h + 1) * HEAD_DIM]
                term = lax.dot_general(q, keys, nt, preferred_element_type=jnp.float32)
                scores.append(term * SCALE + row)
            top = jnp.max(scores[0], axis=1, keepdims=True)
            for s in scores[1:]:
                top = jnp.maximum(top, jnp.max(s, axis=1, keepdims=True))
            total = 0.0
            weighted = 0.0
            for i, s in enumerate(scores):
                w = jnp.exp2(s - top)
                total = total + jnp.sum(w, axis=1, keepdims=True)
                if i == 0:
                    values = vcat[:, head]
                else:
                    values = far[i - 1][0][0:BLOCK, CHUNK + h * HEAD_DIM : CHUNK + (h + 1) * HEAD_DIM]
                weighted = weighted + jnp.dot(
                    w.astype(jnp.bfloat16), values, preferred_element_type=jnp.float32)
            o_ref[:, head] = (weighted / total).astype(jnp.bfloat16)

    def chain_step(step):
        chain_copy(step).wait_recv()
        bit = 1 << step
        theirs = lax.rem(lax.div(pos_ref[window], bit), 2)
        mine = lax.rem(lax.div(column, bit), 2)
        take = jnp.abs(theirs - mine).astype(jnp.float32)
        kept = cur[step].astype(jnp.float32) * (1.0 - take) + rcv[step].astype(jnp.float32) * take
        cur[step + 1] = kept.astype(jnp.bfloat16)
        if step + 1 < steps:
            chain_copy(step + 1).start()
        else:
            send_groups(cur.at[steps], fx_buf, fx_send, fx_recv, lambda copy: copy.start())

    loads[2].wait()
    for turn, chunk in enumerate(ORDER):

        @pl.when(has_two_back)
        def _():
            for part in (0, 1):
                ahead_two(part, chunk).wait_recv()

        @pl.when(forwards)
        def _():
            for part in (0, 1):
                forward(part, chunk).start()

        if turn < steps:
            chain_step(turn)
        if turn + AHEAD < CHUNKS:
            send_chunk(ORDER[turn + AHEAD])
        if turn == AHEAD:
            pass_groups(st_buf, st_recv, st_pass)
        if chunk == FIXED_CHUNK:
            pass_groups(fx_buf, fx_recv, fx_pass)

        @pl.when(has_one_back)
        def _():
            for part in (0, 1):
                ahead_one(part, chunk).wait_recv()

        far = []
        if chunk == STRIDED_CHUNK:
            rest_of_groups(st_buf, st_recv, st_pass)
            for slot in range(groups - 1):
                far.append((st_buf.at[slot], (slot < window).astype(jnp.float32)))
        if chunk == FIXED_CHUNK:
            rest_of_groups(fx_buf, fx_recv, fx_pass)
            for slot in range(groups - 1):
                used = (slot < window) & (slot * stride + pos_ref[slot] < me - LOOKBACK)
                far.append((fx_buf.at[slot], used.astype(jnp.float32)))
            used = window * stride + pos_ref[window] < me - LOOKBACK
            far.append((cur.at[steps], used.astype(jnp.float32)))
        attend(chunk, far)

    @pl.when(has_one_ahead)
    def _():
        keep_copy(1).wait_send()

    @pl.when(has_two_ahead)
    def _():
        keep_copy(2).wait_send()
        for chunk in ORDER:
            for part in (0, 1):
                ahead_two(part, chunk).wait_send()

    @pl.when(is_even | forwards)
    def _():
        for chunk in ORDER:
            for part in (0, 1):
                ahead_one(part, chunk).wait_send()

    for step in range(steps):
        chain_copy(step).wait_send()
    send_groups(st_src, st_buf, st_send, st_recv, lambda copy: copy.wait_send())
    send_groups(cur.at[steps], fx_buf, fx_send, fx_recv, lambda copy: copy.wait_send())
    passed_on(st_buf, st_recv, st_pass)
    passed_on(fx_buf, fx_recv, fx_pass)


def on_device(queries, key_states, value_states, key_keep, summary_pos, *, stride, groups):
    steps = stride.bit_length() - 1
    assert 1 << steps == stride and steps < CHUNKS and groups % 2 == 0
    vmem = pl.BlockSpec(memory_space=pltpu.VMEM)
    hbm = pl.BlockSpec(memory_space=pl.ANY)
    dma = pltpu.SemaphoreType.DMA
    far = (FAR_ROWS, FAR_COLS)
    return pl.pallas_call(
        functools.partial(kernel, stride, groups),
        out_shape=jax.ShapeDtypeStruct((BLOCK, WIDTH), jnp.bfloat16),
        in_specs=[pl.BlockSpec(memory_space=pltpu.SMEM), hbm, hbm, hbm, vmem],
        out_specs=vmem,
        scratch_shapes=[
            pltpu.VMEM((BLOCK, WIDTH), jnp.bfloat16),
            pltpu.VMEM((3 * BLOCK, WIDTH), jnp.bfloat16),
            pltpu.VMEM((3 * BLOCK, WIDTH), jnp.bfloat16),
            pltpu.VMEM((3, 16, BLOCK), jnp.bfloat16),
            pltpu.VMEM((BLOCK, 3 * BLOCK), jnp.float32),
            pltpu.VMEM(far, jnp.bfloat16),
            pltpu.VMEM((groups - 1,) + far, jnp.bfloat16),
            pltpu.VMEM((steps + 1,) + far, jnp.bfloat16),
            pltpu.VMEM((steps,) + far, jnp.bfloat16),
            pltpu.VMEM((groups - 1,) + far, jnp.bfloat16),
            dma((2, 2, CHUNKS)), dma((2, 2, CHUNKS)),
            dma((2,)), dma((2,)),
            dma((steps,)), dma((steps,)),
            dma((groups - 1,)), dma((groups - 1,)), dma((groups - 1,)),
            dma((groups - 1,)), dma((groups - 1,)), dma((groups - 1,)),
            dma((3,)),
        ],
        compiler_params=pltpu.CompilerParams(
            collective_id=0, has_side_effects=True, vmem_limit_bytes=40 * 1024 * 1024),
    )(summary_pos, queries, key_states, value_states, key_keep.reshape(1, BLOCK))


def solution(mesh):
    rows = P(("grp", "seq"), None)
    return jax.shard_map(
        functools.partial(on_device, stride=mesh.shape["seq"], groups=mesh.shape["grp"]),
        mesh=mesh,
        in_specs=(rows, rows, rows, P(("grp", "seq")), P()),
        out_specs=rows,
        check_vma=False,
    )
```

```python
import functools
import math

import jax
import jax.numpy as jnp
from jax import lax
from jax.experimental import pallas as pl
from jax.experimental.pallas import tpu as pltpu
from jax.sharding import PartitionSpec as P

HEADS = 24
HEAD_DIM = 128
FIXED_HEADS = 4
STRIDED_HEADS = 4
LOCAL_HEADS = 16
BLOCK = 128
LOOKBACK = 2
WIDTH = HEADS * HEAD_DIM

CHUNK_HEADS = 4
CHUNK = CHUNK_HEADS * HEAD_DIM
CHUNKS = HEADS // CHUNK_HEADS
FIXED_CHUNK = LOCAL_HEADS // CHUNK_HEADS
STRIDED_CHUNK = (LOCAL_HEADS + FIXED_HEADS) // CHUNK_HEADS
ORDER = tuple(range(FIXED_CHUNK)) + (STRIDED_CHUNK, FIXED_CHUNK)
FAR_ROWS = BLOCK + 16
FAR_COLS = 2 * CHUNK
HALF = FAR_COLS // 2
HALF_HEADS = CHUNK_HEADS // 2
HALF_KEYS = HALF_HEADS * HEAD_DIM

AHEAD = 2
NEG = -1e30
SCALE = math.log2(math.e) / math.sqrt(HEAD_DIM)
MESH = pl.DeviceIdType.MESH


def kernel(
    stride, groups, pos_ref, q_hbm, k_hbm, v_hbm, keep_ref, o_ref,
    q_ref, kcat, vcat, keeps, bias, st_src, st_buf, fx_src, half, rcv, fin, fx_buf,
    halo_send, halo_recv, keep_send, keep_recv, ch_send, ch_recv,
    st_send, st_recv, st_pass, fx_send, fx_recv, fx_pass, load_sem,
):
    steps = stride.bit_length() - 1
    blocks = stride * groups
    window = lax.axis_index("grp")
    column = lax.axis_index("seq")
    me = window * stride + column
    odd = lax.rem(column, 2)
    is_odd = odd == 1
    is_even = odd == 0
    core = lax.rem(window, 2)
    chip = window - core
    own_rows = pl.ds(LOOKBACK * BLOCK, BLOCK)
    loads = [
        pltpu.make_async_copy(src, dst, load_sem.at[i])
        for i, (src, dst) in enumerate(
            ((k_hbm, kcat.at[own_rows]), (v_hbm, vcat.at[own_rows]), (q_hbm, q_ref)))
    ]
    for load in loads:
        load.start()

    def device(block):
        return (lax.div(block, stride), lax.rem(block, stride))

    def partner(step):
        bit = 1 << step
        mine = lax.rem(lax.div(column, bit), 2)
        return (window, column + bit * (1 - 2 * mine))

    def cols(chunk):
        return pl.ds(chunk * CHUNK, CHUNK)

    barrier = pltpu.get_barrier_semaphore()
    greeted = 0
    for away in (-2, -1, 1, 2):
        there = (me + away >= 0) & (me + away < blocks)

        @pl.when(there)
        def _():
            pl.semaphore_signal(barrier, inc=1, device_id=device(me + away), device_id_type=MESH)

        greeted = greeted + there.astype(jnp.int32)
    for step in range(steps):
        pl.semaphore_signal(barrier, inc=1, device_id=partner(step), device_id_type=MESH)
    for away in range(1, groups):
        other = lax.rem(window + away, groups)
        pl.semaphore_signal(barrier, inc=1, device_id=(other, column), device_id_type=MESH)

    keep_row = keep_ref[...].astype(jnp.float32)
    keep_tile = jnp.broadcast_to(keep_row, (16, BLOCK)).astype(jnp.bfloat16)
    keeps[2] = keep_tile
    loads[0].wait()
    loads[1].wait()
    for buf, chunk in ((st_src, STRIDED_CHUNK), (fx_src, FIXED_CHUNK)):
        for i in (0, 1):
            some = pl.ds(chunk * CHUNK + i * HALF_KEYS, HALF_KEYS)
            buf[0:BLOCK, i * HALF : i * HALF + HALF_KEYS] = kcat[own_rows, some]
            buf[0:BLOCK, i * HALF + HALF_KEYS : (i + 1) * HALF] = vcat[own_rows, some]
        for lane in range(0, FAR_COLS, BLOCK):
            buf[BLOCK:FAR_ROWS, lane : lane + BLOCK] = keep_tile

    pl.semaphore_wait(barrier, greeted + (steps + groups - 1))

    def keep_copy(ahead):
        slot = LOOKBACK - ahead
        return pltpu.make_async_remote_copy(
            src_ref=keeps.at[2], dst_ref=keeps.at[slot],
            send_sem=keep_send.at[slot], recv_sem=keep_recv.at[slot],
            device_id=device(jnp.minimum(me + ahead, blocks - 1)), device_id_type=MESH)

    mine_half = pl.ds(pl.multiple_of(odd * HALF, HALF), HALF)
    other_half = pl.ds(pl.multiple_of((1 - odd) * HALF, HALF), HALF)

    def chain_copy(step):
        if step == 0:
            src, dst = fx_src.at[:, other_half], rcv.at[0]
        elif step < steps:
            src, dst = half.at[step - 1], rcv.at[step]
        else:
            src, dst = fin.at[:, mine_half], fin.at[:, mine_half]
        return pltpu.make_async_remote_copy(
            src_ref=src, dst_ref=dst,
            send_sem=ch_send.at[step], recv_sem=ch_recv.at[step],
            device_id=partner(step % steps), device_id_type=MESH)

    def group_copy(src, buf, send_sem, recv_sem, away):
        return pltpu.make_async_remote_copy(
            src_ref=src, dst_ref=buf.at[window],
            send_sem=send_sem.at[away - 1], recv_sem=recv_sem.at[window],
            device_id=(window + away, column), device_id_type=MESH)

    def halo_copy(slot, part, chunk, src, target):
        cat = (kcat, vcat)[part]
        return pltpu.make_async_remote_copy(
            src_ref=src, dst_ref=cat.at[pl.ds(slot * BLOCK, BLOCK), cols(chunk)],
            send_sem=halo_send.at[slot, part, chunk], recv_sem=halo_recv.at[slot, part, chunk],
            device_id=device(target), device_id_type=MESH)

    def own(part, chunk):
        return (kcat, vcat)[part].at[own_rows, cols(chunk)]

    def ahead_two(part, chunk):
        return halo_copy(0, part, chunk, own(part, chunk), me + 2)

    def ahead_one(part, chunk):
        return halo_copy(1, part, chunk, own(part, chunk), me + 1)

    def forward(part, chunk):
        src = (kcat, vcat)[part].at[pl.ds(0, BLOCK), cols(chunk)]
        return halo_copy(1, part, chunk, src, me - 1)

    has_two_ahead = me + 2 < blocks
    has_one_ahead = me + 1 < blocks
    has_two_back = me >= 2
    has_one_back = me >= 1
    forwards = is_odd & has_two_back

    @pl.when(has_one_ahead)
    def _():
        keep_copy(1).start()

    @pl.when(has_two_ahead)
    def _():
        keep_copy(2).start()

    def goes(away):
        if away == 1:
            return core == 0
        return (window + away < groups) & (away % 2 == 0)

    def send_groups(src, buf, send_sem, recv_sem, act):
        for away in range(1, groups):
            if away == 1 or away % 2 == 0:

                @pl.when(goes(away))
                def _():
                    act(group_copy(src, buf, send_sem, recv_sem, away))

    def pass_copy(buf, recv_sem, pass_sem, slot):
        return pltpu.make_async_remote_copy(
            src_ref=buf.at[slot], dst_ref=buf.at[slot],
            send_sem=pass_sem.at[slot], recv_sem=recv_sem.at[slot],
            device_id=(chip + 1 - core, column), device_id_type=MESH)

    def passes(slot):
        return (slot < chip) & (core == slot % 2)

    def pass_groups(buf, recv_sem, pass_sem):
        for slot in range(groups - 2):

            @pl.when(passes(slot))
            def _():
                copy = pass_copy(buf, recv_sem, pass_sem, slot)
                copy.wait_recv()
                copy.start()

    def rest_of_groups(buf, recv_sem, pass_sem):
        for slot in range(groups - 1):

            @pl.when((slot < window) & jnp.logical_not(passes(slot)))
            def _():
                pass_copy(buf, recv_sem, pass_sem, slot).wait_recv()

    def passed_on(buf, recv_sem, pass_sem):
        for slot in range(groups - 2):

            @pl.when(passes(slot))
            def _():
                pass_copy(buf, recv_sem, pass_sem, slot).wait_send()

    chain_copy(0).start()
    send_groups(st_src, st_buf, st_send, st_recv, lambda copy: copy.start())

    def send_chunk(chunk):

        @pl.when(has_two_ahead)
        def _():
            for part in (0, 1):
                ahead_two(part, chunk).start()

        @pl.when(is_even)
        def _():
            for part in (0, 1):
                ahead_one(part, chunk).start()

    for chunk in ORDER[:AHEAD]:
        send_chunk(chunk)

    @pl.when(me < 2)
    def _():
        keeps[0] = jnp.zeros((16, BLOCK), jnp.bfloat16)
        kcat[0:BLOCK, :] = jnp.zeros((BLOCK, WIDTH), jnp.bfloat16)
        vcat[0:BLOCK, :] = jnp.zeros((BLOCK, WIDTH), jnp.bfloat16)

    @pl.when(me < 1)
    def _():
        keeps[1] = jnp.zeros((16, BLOCK), jnp.bfloat16)
        kcat[BLOCK : 2 * BLOCK, :] = jnp.zeros((BLOCK, WIDTH), jnp.bfloat16)
        vcat[BLOCK : 2 * BLOCK, :] = jnp.zeros((BLOCK, WIDTH), jnp.bfloat16)

    for slot in range(groups - 1):

        @pl.when(slot >= window)
        def _():
            st_buf[slot] = jnp.zeros((FAR_ROWS, FAR_COLS), jnp.bfloat16)
            fx_buf[slot] = jnp.zeros((FAR_ROWS, FAR_COLS), jnp.bfloat16)

    @pl.when(has_two_back)
    def _():
        keep_copy(2).wait_recv()

    @pl.when(has_one_back)
    def _():
        keep_copy(1).wait_recv()

    def as_bias(flags):
        return jnp.where(flags > 0.5, 0.0, NEG)

    for slot in (0, 1):
        row = as_bias(keeps[slot][0:1, :].astype(jnp.float32))
        bias[:, slot * BLOCK : (slot + 1) * BLOCK] = jnp.broadcast_to(row, (BLOCK, BLOCK))
    query_ids = lax.broadcasted_iota(jnp.int32, (BLOCK, BLOCK), 0)
    key_ids = lax.broadcasted_iota(jnp.int32, (BLOCK, BLOCK), 1)
    flags = jnp.where(key_ids == query_ids, 1.0, jnp.broadcast_to(keep_row, (BLOCK, BLOCK)))
    bias[:, 2 * BLOCK :] = as_bias(jnp.where(key_ids <= query_ids, flags, 0.0))

    def attend(chunk, far):
        rows = []
        for buf, flag in far:
            keep = buf[BLOCK : BLOCK + 16, 0:BLOCK].astype(jnp.float32)[0:1, :]
            rows.append(as_bias(keep * flag))
        for h in range(CHUNK_HEADS):
            at = chunk * CHUNK + h * HEAD_DIM
            head = pl.ds(at, HEAD_DIM)
            far_at = h // HALF_HEADS * HALF + h % HALF_HEADS * HEAD_DIM
            q = q_ref[:, head]
            nt = (((1,), (1,)), ((), ()))
            near = lax.dot_general(q, kcat[:, head], nt, preferred_element_type=jnp.float32)
            scores = [near * SCALE + bias[...]]
            for (buf, _), row in zip(far, rows):
                keys = buf[0:BLOCK, far_at : far_at + HEAD_DIM]
                term = lax.dot_general(q, keys, nt, preferred_element_type=jnp.float32)
                scores.append(term * SCALE + row)
            top = jnp.max(scores[0], axis=1, keepdims=True)
            for s in scores[1:]:
                top = jnp.maximum(top, jnp.max(s, axis=1, keepdims=True))
            total = 0.0
            weighted = 0.0
            for i, s in enumerate(scores):
                w = jnp.exp2(s - top)
                total = total + jnp.sum(w, axis=1, keepdims=True)
                if i == 0:
                    values = vcat[:, head]
                else:
                    far_values = far_at + HALF_KEYS
                    values = far[i - 1][0][0:BLOCK, far_values : far_values + HEAD_DIM]
                weighted = weighted + jnp.dot(
                    w.astype(jnp.bfloat16), values, preferred_element_type=jnp.float32)
            o_ref[:, head] = (weighted / total).astype(jnp.bfloat16)

    def chain_step(step):
        chain_copy(step).wait_recv()
        if step == steps:
            send_groups(fin, fx_buf, fx_send, fx_recv, lambda copy: copy.start())
            return
        bit = 1 << step
        theirs = lax.rem(lax.div(pos_ref[window], bit), 2)
        mine = lax.rem(lax.div(column, bit), 2)
        take = jnp.abs(theirs - mine).astype(jnp.float32)
        held = fx_src[:, mine_half] if step == 0 else half[step - 1]
        kept = held.astype(jnp.float32) * (1.0 - take) + rcv[step].astype(jnp.float32) * take
        if step + 1 < steps:
            half[step] = kept.astype(jnp.bfloat16)
        else:
            fin[:, mine_half] = kept.astype(jnp.bfloat16)
        chain_copy(step + 1).start()

    def own_sent(chunk):

        @pl.when(has_two_ahead)
        def _():
            for part in (0, 1):
                ahead_two(part, chunk).wait_send()

        @pl.when(is_even)
        def _():
            for part in (0, 1):
                ahead_one(part, chunk).wait_send()

    loads[2].wait()
    for turn, chunk in enumerate(ORDER):

        @pl.when(has_two_back)
        def _():
            for part in (0, 1):
                ahead_two(part, chunk).wait_recv()

        @pl.when(forwards)
        def _():
            for part in (0, 1):
                forward(part, chunk).start()

        if turn <= steps:
            chain_step(turn)
        if turn + AHEAD < CHUNKS:
            own_sent(chunk)
            send_chunk(ORDER[turn + AHEAD])
        if turn == AHEAD:
            pass_groups(st_buf, st_recv, st_pass)
        if chunk == FIXED_CHUNK:
            pass_groups(fx_buf, fx_recv, fx_pass)

        @pl.when(has_one_back)
        def _():
            for part in (0, 1):
                ahead_one(part, chunk).wait_recv()

        far = []
        if chunk == STRIDED_CHUNK:
            rest_of_groups(st_buf, st_recv, st_pass)
            for slot in range(groups - 1):
                far.append((st_buf.at[slot], (slot < window).astype(jnp.float32)))
        if chunk == FIXED_CHUNK:
            rest_of_groups(fx_buf, fx_recv, fx_pass)
            for slot in range(groups - 1):
                used = (slot < window) & (slot * stride + pos_ref[slot] < me - LOOKBACK)
                far.append((fx_buf.at[slot], used.astype(jnp.float32)))
            used = window * stride + pos_ref[window] < me - LOOKBACK
            far.append((fin, used.astype(jnp.float32)))
        attend(chunk, far)

    @pl.when(has_one_ahead)
    def _():
        keep_copy(1).wait_send()

    @pl.when(has_two_ahead)
    def _():
        keep_copy(2).wait_send()

    for chunk in ORDER[CHUNKS - AHEAD :]:
        own_sent(chunk)

    @pl.when(forwards)
    def _():
        for chunk in ORDER:
            for part in (0, 1):
                forward(part, chunk).wait_send()

    for step in range(steps + 1):
        chain_copy(step).wait_send()
    send_groups(st_src, st_buf, st_send, st_recv, lambda copy: copy.wait_send())
    send_groups(fin, fx_buf, fx_send, fx_recv, lambda copy: copy.wait_send())
    passed_on(st_buf, st_recv, st_pass)
    passed_on(fx_buf, fx_recv, fx_pass)


def on_device(queries, key_states, value_states, key_keep, summary_pos, *, stride, groups):
    steps = stride.bit_length() - 1
    assert 1 << steps == stride and 1 < steps < CHUNKS and groups % 2 == 0
    vmem = pl.BlockSpec(memory_space=pltpu.VMEM)
    hbm = pl.BlockSpec(memory_space=pl.ANY)
    dma = pltpu.SemaphoreType.DMA
    far = (FAR_ROWS, FAR_COLS)
    return pl.pallas_call(
        functools.partial(kernel, stride, groups),
        out_shape=jax.ShapeDtypeStruct((BLOCK, WIDTH), jnp.bfloat16),
        in_specs=[pl.BlockSpec(memory_space=pltpu.SMEM), hbm, hbm, hbm, vmem],
        out_specs=vmem,
        scratch_shapes=[
            pltpu.VMEM((BLOCK, WIDTH), jnp.bfloat16),
            pltpu.VMEM((3 * BLOCK, WIDTH), jnp.bfloat16),
            pltpu.VMEM((3 * BLOCK, WIDTH), jnp.bfloat16),
            pltpu.VMEM((3, 16, BLOCK), jnp.bfloat16),
            pltpu.VMEM((BLOCK, 3 * BLOCK), jnp.float32),
            pltpu.VMEM(far, jnp.bfloat16),
            pltpu.VMEM((groups - 1,) + far, jnp.bfloat16),
            pltpu.VMEM(far, jnp.bfloat16),
            pltpu.VMEM((steps - 1, FAR_ROWS, HALF), jnp.bfloat16),
            pltpu.VMEM((steps, FAR_ROWS, HALF), jnp.bfloat16),
            pltpu.VMEM(far, jnp.bfloat16),
            pltpu.VMEM((groups - 1,) + far, jnp.bfloat16),
            dma((2, 2, CHUNKS)), dma((2, 2, CHUNKS)),
            dma((2,)), dma((2,)),
            dma((steps + 1,)), dma((steps + 1,)),
            dma((groups - 1,)), dma((groups - 1,)), dma((groups - 1,)),
            dma((groups - 1,)), dma((groups - 1,)), dma((groups - 1,)),
            dma((3,)),
        ],
        compiler_params=pltpu.CompilerParams(
            collective_id=0, has_side_effects=True, vmem_limit_bytes=40 * 1024 * 1024),
    )(summary_pos, queries, key_states, value_states, key_keep.reshape(1, BLOCK))


def solution(mesh):
    rows = P(("grp", "seq"), None)
    return jax.shard_map(
        functools.partial(on_device, stride=mesh.shape["seq"], groups=mesh.shape["grp"]),
        mesh=mesh,
        in_specs=(rows, rows, rows, P(("grp", "seq")), P()),
        out_specs=rows,
        check_vma=False,
    )
```

```python
import functools
import math

import jax
import jax.numpy as jnp
from jax import lax
from jax.experimental import pallas as pl
from jax.experimental.pallas import tpu as pltpu
from jax.sharding import PartitionSpec as P

HEADS = 24
HEAD_DIM = 128
FIXED_HEADS = 4
STRIDED_HEADS = 4
LOCAL_HEADS = 16
BLOCK = 128
LOOKBACK = 2
WIDTH = HEADS * HEAD_DIM

CHUNK_HEADS = 4
CHUNK = CHUNK_HEADS * HEAD_DIM
CHUNKS = HEADS // CHUNK_HEADS
FIXED_CHUNK = LOCAL_HEADS // CHUNK_HEADS
STRIDED_CHUNK = (LOCAL_HEADS + FIXED_HEADS) // CHUNK_HEADS
ORDER = tuple(range(FIXED_CHUNK)) + (STRIDED_CHUNK, FIXED_CHUNK)
FAR_ROWS = BLOCK + 16
FAR_COLS = 2 * CHUNK
HALF = FAR_COLS // 2
HALF_HEADS = CHUNK_HEADS // 2
HALF_KEYS = HALF_HEADS * HEAD_DIM

AHEAD = 2
NEG = -1e30
SCALE = math.log2(math.e) / math.sqrt(HEAD_DIM)
MESH = pl.DeviceIdType.MESH


def kernel(
    stride, groups, pos_ref, q_hbm, k_hbm, v_hbm, keep_ref, o_ref,
    q_ref, kcat, vcat, keeps, bias, st_src, st_buf, fx_src, half, rcv, fin, fx_buf,
    halo_send, halo_recv, keep_send, keep_recv, ch_send, ch_recv,
    st_send, st_recv, st_pass, fx_send, fx_recv, fx_pass, load_sem,
):
    steps = stride.bit_length() - 1
    blocks = stride * groups
    window = lax.axis_index("grp")
    column = lax.axis_index("seq")
    me = window * stride + column
    odd = lax.rem(column, 2)
    is_odd = odd == 1
    is_even = odd == 0
    core = lax.rem(window, 2)
    chip = window - core
    own_rows = pl.ds(LOOKBACK * BLOCK, BLOCK)
    loads = [
        pltpu.make_async_copy(src, dst, load_sem.at[i])
        for i, (src, dst) in enumerate(
            ((k_hbm, kcat.at[own_rows]), (v_hbm, vcat.at[own_rows]), (q_hbm, q_ref)))
    ]
    for load in loads:
        load.start()

    def device(block):
        return (lax.div(block, stride), lax.rem(block, stride))

    def partner(step):
        bit = 1 << step
        mine = lax.rem(lax.div(column, bit), 2)
        return (window, column + bit * (1 - 2 * mine))

    def cols(chunk):
        return pl.ds(chunk * CHUNK, CHUNK)

    barrier = pltpu.get_barrier_semaphore()
    greeted = 0
    for away in (-2, -1, 1, 2):
        there = (me + away >= 0) & (me + away < blocks)

        @pl.when(there)
        def _():
            pl.semaphore_signal(barrier, inc=1, device_id=device(me + away), device_id_type=MESH)

        greeted = greeted + there.astype(jnp.int32)
    for step in range(steps):
        pl.semaphore_signal(barrier, inc=1, device_id=partner(step), device_id_type=MESH)
    for away in range(1, groups):
        other = lax.rem(window + away, groups)
        pl.semaphore_signal(barrier, inc=1, device_id=(other, column), device_id_type=MESH)

    keep_row = keep_ref[...].astype(jnp.float32)
    keep_tile = jnp.broadcast_to(keep_row, (16, BLOCK)).astype(jnp.bfloat16)
    keeps[2] = keep_tile
    loads[0].wait()
    loads[1].wait()
    for buf, chunk in ((st_src, STRIDED_CHUNK), (fx_src, FIXED_CHUNK)):
        for i in (0, 1):
            some = pl.ds(chunk * CHUNK + i * HALF_KEYS, HALF_KEYS)
            buf[0:BLOCK, i * HALF : i * HALF + HALF_KEYS] = kcat[own_rows, some]
            buf[0:BLOCK, i * HALF + HALF_KEYS : (i + 1) * HALF] = vcat[own_rows, some]
        for lane in range(0, FAR_COLS, BLOCK):
            buf[BLOCK:FAR_ROWS, lane : lane + BLOCK] = keep_tile

    pl.semaphore_wait(barrier, greeted + (steps + groups - 1))

    def keep_copy(ahead):
        slot = LOOKBACK - ahead
        return pltpu.make_async_remote_copy(
            src_ref=keeps.at[2], dst_ref=keeps.at[slot],
            send_sem=keep_send.at[slot], recv_sem=keep_recv.at[slot],
            device_id=device(jnp.minimum(me + ahead, blocks - 1)), device_id_type=MESH)

    mine_half = pl.ds(pl.multiple_of(odd * HALF, HALF), HALF)
    other_half = pl.ds(pl.multiple_of((1 - odd) * HALF, HALF), HALF)

    def chain_copy(step):
        if step == 0:
            src, dst = fx_src.at[:, other_half], rcv.at[0]
        elif step < steps:
            src, dst = half.at[step - 1], rcv.at[step]
        else:
            src, dst = fin.at[:, mine_half], fin.at[:, mine_half]
        return pltpu.make_async_remote_copy(
            src_ref=src, dst_ref=dst,
            send_sem=ch_send.at[step], recv_sem=ch_recv.at[step],
            device_id=partner(step % steps), device_id_type=MESH)

    def group_copy(src, buf, send_sem, recv_sem, away):
        return pltpu.make_async_remote_copy(
            src_ref=src, dst_ref=buf.at[window],
            send_sem=send_sem.at[away - 1], recv_sem=recv_sem.at[window],
            device_id=(window + away, column), device_id_type=MESH)

    def halo_copy(slot, part, chunk, src, target):
        cat = (kcat, vcat)[part]
        return pltpu.make_async_remote_copy(
            src_ref=src, dst_ref=cat.at[pl.ds(slot * BLOCK, BLOCK), cols(chunk)],
            send_sem=halo_send.at[slot, part, chunk], recv_sem=halo_recv.at[slot, part, chunk],
            device_id=device(target), device_id_type=MESH)

    def own(part, chunk):
        return (kcat, vcat)[part].at[own_rows, cols(chunk)]

    def ahead_two(part, chunk):
        return halo_copy(0, part, chunk, own(part, chunk), me + 2)

    def ahead_one(part, chunk):
        return halo_copy(1, part, chunk, own(part, chunk), me + 1)

    def forward(part, chunk):
        src = (kcat, vcat)[part].at[pl.ds(0, BLOCK), cols(chunk)]
        return halo_copy(1, part, chunk, src, me - 1)

    has_two_ahead = me + 2 < blocks
    has_one_ahead = me + 1 < blocks
    has_two_back = me >= 2
    has_one_back = me >= 1
    forwards = is_odd & has_two_back

    @pl.when(has_one_ahead)
    def _():
        keep_copy(1).start()

    @pl.when(has_two_ahead)
    def _():
        keep_copy(2).start()

    def goes(away):
        if away == 1:
            return core == 0
        return (window + away < groups) & (away % 2 == 0)

    def send_groups(src, buf, send_sem, recv_sem, act):
        for away in range(1, groups):
            if away == 1 or away % 2 == 0:

                @pl.when(goes(away))
                def _():
                    act(group_copy(src, buf, send_sem, recv_sem, away))

    def pass_copy(buf, recv_sem, pass_sem, slot):
        return pltpu.make_async_remote_copy(
            src_ref=buf.at[slot], dst_ref=buf.at[slot],
            send_sem=pass_sem.at[slot], recv_sem=recv_sem.at[slot],
            device_id=(chip + 1 - core, column), device_id_type=MESH)

    def passes(slot):
        return (slot < chip) & (core == slot % 2)

    def pass_groups(buf, recv_sem, pass_sem):
        for slot in range(groups - 2):

            @pl.when(passes(slot))
            def _():
                copy = pass_copy(buf, recv_sem, pass_sem, slot)
                copy.wait_recv()
                copy.start()

    def rest_of_groups(buf, recv_sem, pass_sem):
        for slot in range(groups - 1):

            @pl.when((slot < window) & jnp.logical_not(passes(slot)))
            def _():
                pass_copy(buf, recv_sem, pass_sem, slot).wait_recv()

    def passed_on(buf, recv_sem, pass_sem):
        for slot in range(groups - 2):

            @pl.when(passes(slot))
            def _():
                pass_copy(buf, recv_sem, pass_sem, slot).wait_send()

    chain_copy(0).start()
    send_groups(st_src, st_buf, st_send, st_recv, lambda copy: copy.start())

    def send_chunk(chunk):

        @pl.when(has_two_ahead)
        def _():
            for part in (0, 1):
                ahead_two(part, chunk).start()

        @pl.when(is_even)
        def _():
            for part in (0, 1):
                ahead_one(part, chunk).start()

    for chunk in ORDER[:AHEAD]:
        send_chunk(chunk)

    @pl.when(me < 2)
    def _():
        keeps[0] = jnp.zeros((16, BLOCK), jnp.bfloat16)
        kcat[0:BLOCK, :] = jnp.zeros((BLOCK, WIDTH), jnp.bfloat16)
        vcat[0:BLOCK, :] = jnp.zeros((BLOCK, WIDTH), jnp.bfloat16)

    @pl.when(me < 1)
    def _():
        keeps[1] = jnp.zeros((16, BLOCK), jnp.bfloat16)
        kcat[BLOCK : 2 * BLOCK, :] = jnp.zeros((BLOCK, WIDTH), jnp.bfloat16)
        vcat[BLOCK : 2 * BLOCK, :] = jnp.zeros((BLOCK, WIDTH), jnp.bfloat16)

    for slot in range(groups - 1):

        @pl.when(slot >= window)
        def _():
            st_buf[slot] = jnp.zeros((FAR_ROWS, FAR_COLS), jnp.bfloat16)
            fx_buf[slot] = jnp.zeros((FAR_ROWS, FAR_COLS), jnp.bfloat16)

    @pl.when(has_two_back)
    def _():
        keep_copy(2).wait_recv()

    @pl.when(has_one_back)
    def _():
        keep_copy(1).wait_recv()

    def as_bias(flags):
        return jnp.where(flags > 0.5, 0.0, NEG)

    for slot in (0, 1):
        row = as_bias(keeps[slot][0:1, :].astype(jnp.float32))
        bias[:, slot * BLOCK : (slot + 1) * BLOCK] = jnp.broadcast_to(row, (BLOCK, BLOCK))
    query_ids = lax.broadcasted_iota(jnp.int32, (BLOCK, BLOCK), 0)
    key_ids = lax.broadcasted_iota(jnp.int32, (BLOCK, BLOCK), 1)
    flags = jnp.where(key_ids == query_ids, 1.0, jnp.broadcast_to(keep_row, (BLOCK, BLOCK)))
    bias[:, 2 * BLOCK :] = as_bias(jnp.where(key_ids <= query_ids, flags, 0.0))

    def attend(chunk, far):
        rows = []
        for buf, flag in far:
            keep = buf[BLOCK : BLOCK + 16, 0:BLOCK].astype(jnp.float32)[0:1, :]
            rows.append(as_bias(keep * flag))
        for h in range(CHUNK_HEADS):
            at = chunk * CHUNK + h * HEAD_DIM
            head = pl.ds(at, HEAD_DIM)
            far_at = h // HALF_HEADS * HALF + h % HALF_HEADS * HEAD_DIM
            q = q_ref[:, head]
            nt = (((1,), (1,)), ((), ()))
            near = lax.dot_general(q, kcat[:, head], nt, preferred_element_type=jnp.float32)
            scores = [near * SCALE + bias[...]]
            for (buf, _), row in zip(far, rows):
                keys = buf[0:BLOCK, far_at : far_at + HEAD_DIM]
                term = lax.dot_general(q, keys, nt, preferred_element_type=jnp.float32)
                scores.append(term * SCALE + row)
            top = jnp.max(scores[0], axis=1, keepdims=True)
            for s in scores[1:]:
                top = jnp.maximum(top, jnp.max(s, axis=1, keepdims=True))
            total = 0.0
            weighted = 0.0
            for i, s in enumerate(scores):
                w = jnp.exp2(s - top)
                total = total + jnp.sum(w, axis=1, keepdims=True)
                if i == 0:
                    values = vcat[:, head]
                else:
                    far_values = far_at + HALF_KEYS
                    values = far[i - 1][0][0:BLOCK, far_values : far_values + HEAD_DIM]
                weighted = weighted + jnp.dot(
                    w.astype(jnp.bfloat16), values, preferred_element_type=jnp.float32)
            o_ref[:, head] = (weighted / total).astype(jnp.bfloat16)

    def chain_step(step):
        chain_copy(step).wait_recv()
        if step == steps:
            send_groups(fin, fx_buf, fx_send, fx_recv, lambda copy: copy.start())
            return
        bit = 1 << step
        theirs = lax.rem(lax.div(pos_ref[window], bit), 2)
        mine = lax.rem(lax.div(column, bit), 2)
        take = jnp.abs(theirs - mine).astype(jnp.float32)
        held = fx_src[:, mine_half] if step == 0 else half[step - 1]
        kept = held.astype(jnp.float32) * (1.0 - take) + rcv[step].astype(jnp.float32) * take
        if step + 1 < steps:
            half[step] = kept.astype(jnp.bfloat16)
        else:
            fin[:, mine_half] = kept.astype(jnp.bfloat16)
        chain_copy(step + 1).start()

    def own_sent(chunk):

        @pl.when(has_two_ahead)
        def _():
            for part in (0, 1):
                ahead_two(part, chunk).wait_send()

        @pl.when(is_even)
        def _():
            for part in (0, 1):
                ahead_one(part, chunk).wait_send()

    loads[2].wait()
    for turn, chunk in enumerate(ORDER):
        if turn + AHEAD < CHUNKS:
            own_sent(chunk)
            send_chunk(ORDER[turn + AHEAD])

        @pl.when(has_two_back)
        def _():
            for part in (0, 1):
                ahead_two(part, chunk).wait_recv()

        @pl.when(forwards)
        def _():
            for part in (0, 1):
                forward(part, chunk).start()

        if steps == CHUNKS - 1 == turn:
            chain_step(turn)
        if turn == AHEAD:
            pass_groups(st_buf, st_recv, st_pass)
        if chunk == FIXED_CHUNK:
            pass_groups(fx_buf, fx_recv, fx_pass)

        @pl.when(has_one_back)
        def _():
            for part in (0, 1):
                ahead_one(part, chunk).wait_recv()

        far = []
        if chunk == STRIDED_CHUNK:
            rest_of_groups(st_buf, st_recv, st_pass)
            for slot in range(groups - 1):
                far.append((st_buf.at[slot], (slot < window).astype(jnp.float32)))
        if chunk == FIXED_CHUNK:
            rest_of_groups(fx_buf, fx_recv, fx_pass)
            for slot in range(groups - 1):
                used = (slot < window) & (slot * stride + pos_ref[slot] < me - LOOKBACK)
                far.append((fx_buf.at[slot], used.astype(jnp.float32)))
            used = window * stride + pos_ref[window] < me - LOOKBACK
            far.append((fin, used.astype(jnp.float32)))
        if turn <= steps and turn < CHUNKS - 1:
            chain_step(turn)
        attend(chunk, far)

    @pl.when(has_one_ahead)
    def _():
        keep_copy(1).wait_send()

    @pl.when(has_two_ahead)
    def _():
        keep_copy(2).wait_send()

    for chunk in ORDER[CHUNKS - AHEAD :]:
        own_sent(chunk)

    @pl.when(forwards)
    def _():
        for chunk in ORDER:
            for part in (0, 1):
                forward(part, chunk).wait_send()

    for step in range(steps + 1):
        chain_copy(step).wait_send()
    send_groups(st_src, st_buf, st_send, st_recv, lambda copy: copy.wait_send())
    send_groups(fin, fx_buf, fx_send, fx_recv, lambda copy: copy.wait_send())
    passed_on(st_buf, st_recv, st_pass)
    passed_on(fx_buf, fx_recv, fx_pass)


def on_device(queries, key_states, value_states, key_keep, summary_pos, *, stride, groups):
    steps = stride.bit_length() - 1
    assert 1 << steps == stride and 1 < steps < CHUNKS and groups % 2 == 0
    vmem = pl.BlockSpec(memory_space=pltpu.VMEM)
    hbm = pl.BlockSpec(memory_space=pl.ANY)
    dma = pltpu.SemaphoreType.DMA
    far = (FAR_ROWS, FAR_COLS)
    return pl.pallas_call(
        functools.partial(kernel, stride, groups),
        out_shape=jax.ShapeDtypeStruct((BLOCK, WIDTH), jnp.bfloat16),
        in_specs=[pl.BlockSpec(memory_space=pltpu.SMEM), hbm, hbm, hbm, vmem],
        out_specs=vmem,
        scratch_shapes=[
            pltpu.VMEM((BLOCK, WIDTH), jnp.bfloat16),
            pltpu.VMEM((3 * BLOCK, WIDTH), jnp.bfloat16),
            pltpu.VMEM((3 * BLOCK, WIDTH), jnp.bfloat16),
            pltpu.VMEM((3, 16, BLOCK), jnp.bfloat16),
            pltpu.VMEM((BLOCK, 3 * BLOCK), jnp.float32),
            pltpu.VMEM(far, jnp.bfloat16),
            pltpu.VMEM((groups - 1,) + far, jnp.bfloat16),
            pltpu.VMEM(far, jnp.bfloat16),
            pltpu.VMEM((steps - 1, FAR_ROWS, HALF), jnp.bfloat16),
            pltpu.VMEM((steps, FAR_ROWS, HALF), jnp.bfloat16),
            pltpu.VMEM(far, jnp.bfloat16),
            pltpu.VMEM((groups - 1,) + far, jnp.bfloat16),
            dma((2, 2, CHUNKS)), dma((2, 2, CHUNKS)),
            dma((2,)), dma((2,)),
            dma((steps + 1,)), dma((steps + 1,)),
            dma((groups - 1,)), dma((groups - 1,)), dma((groups - 1,)),
            dma((groups - 1,)), dma((groups - 1,)), dma((groups - 1,)),
            dma((3,)),
        ],
        compiler_params=pltpu.CompilerParams(
            collective_id=0, has_side_effects=True, vmem_limit_bytes=40 * 1024 * 1024),
    )(summary_pos, queries, key_states, value_states, key_keep.reshape(1, BLOCK))


def solution(mesh):
    rows = P(("grp", "seq"), None)
    return jax.shard_map(
        functools.partial(on_device, stride=mesh.shape["seq"], groups=mesh.shape["grp"]),
        mesh=mesh,
        in_specs=(rows, rows, rows, P(("grp", "seq")), P()),
        out_specs=rows,
        check_vma=False,
    )
```

```python
import functools
import math

import jax
import jax.numpy as jnp
from jax import lax
from jax.experimental import pallas as pl
from jax.experimental.pallas import tpu as pltpu
from jax.sharding import PartitionSpec as P

HEADS = 24
HEAD_DIM = 128
FIXED_HEADS = 4
STRIDED_HEADS = 4
LOCAL_HEADS = 16
BLOCK = 128
LOOKBACK = 2
WIDTH = HEADS * HEAD_DIM

CHUNK_HEADS = 2
CHUNK = CHUNK_HEADS * HEAD_DIM
CHUNKS = HEADS // CHUNK_HEADS
FIXED_CHUNK = LOCAL_HEADS // CHUNK_HEADS
STRIDED_CHUNK = (LOCAL_HEADS + FIXED_HEADS) // CHUNK_HEADS
ORDER = tuple(range(FIXED_CHUNK)) + tuple(range(STRIDED_CHUNK, CHUNKS)) + tuple(range(FIXED_CHUNK, STRIDED_CHUNK))
FAR_HEADS = 4
FAR_ROWS = BLOCK + 16
FAR_COLS = 2 * FAR_HEADS * HEAD_DIM
HALF = FAR_COLS // 2
HALF_HEADS = FAR_HEADS // 2
HALF_KEYS = HALF_HEADS * HEAD_DIM

AHEAD = 3
NEG = -1e30
SCALE = math.log2(math.e) / math.sqrt(HEAD_DIM)
MESH = pl.DeviceIdType.MESH


def kernel(
    stride, groups, pos_ref, q_hbm, k_hbm, v_hbm, keep_ref, o_ref,
    q_ref, kcat, vcat, keeps, bias, st_src, st_buf, fx_src, half, rcv, fin, fx_buf,
    halo_send, halo_recv, keep_send, keep_recv, ch_send, ch_recv,
    st_send, st_recv, st_pass, fx_send, fx_recv, fx_pass, load_sem,
):
    steps = stride.bit_length() - 1
    blocks = stride * groups
    window = lax.axis_index("grp")
    column = lax.axis_index("seq")
    me = window * stride + column
    odd = lax.rem(column, 2)
    is_odd = odd == 1
    is_even = odd == 0
    core = lax.rem(window, 2)
    chip = window - core
    own_rows = pl.ds(LOOKBACK * BLOCK, BLOCK)
    loads = [
        pltpu.make_async_copy(src, dst, load_sem.at[i])
        for i, (src, dst) in enumerate(
            ((k_hbm, kcat.at[own_rows]), (v_hbm, vcat.at[own_rows]), (q_hbm, q_ref)))
    ]
    for load in loads:
        load.start()

    def device(block):
        return (lax.div(block, stride), lax.rem(block, stride))

    def partner(step):
        bit = 1 << step
        mine = lax.rem(lax.div(column, bit), 2)
        return (window, column + bit * (1 - 2 * mine))

    def cols(chunk):
        return pl.ds(chunk * CHUNK, CHUNK)

    barrier = pltpu.get_barrier_semaphore()
    greeted = 0
    for away in (-2, -1, 1, 2):
        there = (me + away >= 0) & (me + away < blocks)

        @pl.when(there)
        def _():
            pl.semaphore_signal(barrier, inc=1, device_id=device(me + away), device_id_type=MESH)

        greeted = greeted + there.astype(jnp.int32)
    for step in range(steps):
        pl.semaphore_signal(barrier, inc=1, device_id=partner(step), device_id_type=MESH)
    for away in range(1, groups):
        other = lax.rem(window + away, groups)
        pl.semaphore_signal(barrier, inc=1, device_id=(other, column), device_id_type=MESH)

    keep_row = keep_ref[...].astype(jnp.float32)
    keep_tile = jnp.broadcast_to(keep_row, (16, BLOCK)).astype(jnp.bfloat16)
    keeps[2] = keep_tile
    loads[0].wait()
    loads[1].wait()
    for buf, first in ((st_src, LOCAL_HEADS + FIXED_HEADS), (fx_src, LOCAL_HEADS)):
        for i in (0, 1):
            some = pl.ds(first * HEAD_DIM + i * HALF_KEYS, HALF_KEYS)
            buf[0:BLOCK, i * HALF : i * HALF + HALF_KEYS] = kcat[own_rows, some]
            buf[0:BLOCK, i * HALF + HALF_KEYS : (i + 1) * HALF] = vcat[own_rows, some]
        for lane in range(0, FAR_COLS, BLOCK):
            buf[BLOCK:FAR_ROWS, lane : lane + BLOCK] = keep_tile

    pl.semaphore_wait(barrier, greeted + (steps + groups - 1))

    def keep_copy(ahead):
        slot = LOOKBACK - ahead
        return pltpu.make_async_remote_copy(
            src_ref=keeps.at[2], dst_ref=keeps.at[slot],
            send_sem=keep_send.at[slot], recv_sem=keep_recv.at[slot],
            device_id=device(jnp.minimum(me + ahead, blocks - 1)), device_id_type=MESH)

    mine_half = pl.ds(pl.multiple_of(odd * HALF, HALF), HALF)
    other_half = pl.ds(pl.multiple_of((1 - odd) * HALF, HALF), HALF)

    def chain_copy(step):
        if step == 0:
            src, dst = fx_src.at[:, other_half], rcv.at[0]
        elif step < steps:
            src, dst = half.at[step - 1], rcv.at[step]
        else:
            src, dst = fin.at[:, mine_half], fin.at[:, mine_half]
        return pltpu.make_async_remote_copy(
            src_ref=src, dst_ref=dst,
            send_sem=ch_send.at[step], recv_sem=ch_recv.at[step],
            device_id=partner(step % steps), device_id_type=MESH)

    def group_copy(src, buf, send_sem, recv_sem, away):
        return pltpu.make_async_remote_copy(
            src_ref=src, dst_ref=buf.at[window],
            send_sem=send_sem.at[away - 1], recv_sem=recv_sem.at[window],
            device_id=(window + away, column), device_id_type=MESH)

    def halo_copy(slot, part, chunk, src, target):
        cat = (kcat, vcat)[part]
        return pltpu.make_async_remote_copy(
            src_ref=src, dst_ref=cat.at[pl.ds(slot * BLOCK, BLOCK), cols(chunk)],
            send_sem=halo_send.at[slot, part, chunk], recv_sem=halo_recv.at[slot, part, chunk],
            device_id=device(target), device_id_type=MESH)

    def own(part, chunk):
        return (kcat, vcat)[part].at[own_rows, cols(chunk)]

    def ahead_two(part, chunk):
        return halo_copy(0, part, chunk, own(part, chunk), me + 2)

    def ahead_one(part, chunk):
        return halo_copy(1, part, chunk, own(part, chunk), me + 1)

    def forward(part, chunk):
        src = (kcat, vcat)[part].at[pl.ds(0, BLOCK), cols(chunk)]
        return halo_copy(1, part, chunk, src, me - 1)

    has_two_ahead = me + 2 < blocks
    has_one_ahead = me + 1 < blocks
    has_two_back = me >= 2
    has_one_back = me >= 1
    forwards = is_odd & has_two_back

    @pl.when(has_one_ahead)
    def _():
        keep_copy(1).start()

    @pl.when(has_two_ahead)
    def _():
        keep_copy(2).start()

    def goes(away):
        if away == 1:
            return core == 0
        return (window + away < groups) & (away % 2 == 0)

    def send_groups(src, buf, send_sem, recv_sem, act):
        for away in range(1, groups):
            if away == 1 or away % 2 == 0:

                @pl.when(goes(away))
                def _():
                    act(group_copy(src, buf, send_sem, recv_sem, away))

    def pass_copy(buf, recv_sem, pass_sem, slot):
        return pltpu.make_async_remote_copy(
            src_ref=buf.at[slot], dst_ref=buf.at[slot],
            send_sem=pass_sem.at[slot], recv_sem=recv_sem.at[slot],
            device_id=(chip + 1 - core, column), device_id_type=MESH)

    def passes(slot):
        return (slot < chip) & (core == slot % 2)

    def pass_groups(buf, recv_sem, pass_sem):
        for slot in range(groups - 2):

            @pl.when(passes(slot))
            def _():
                copy = pass_copy(buf, recv_sem, pass_sem, slot)
                copy.wait_recv()
                copy.start()

    def rest_of_groups(buf, recv_sem, pass_sem):
        for slot in range(groups - 1):

            @pl.when((slot < window) & jnp.logical_not(passes(slot)))
            def _():
                pass_copy(buf, recv_sem, pass_sem, slot).wait_recv()

    def passed_on(buf, recv_sem, pass_sem):
        for slot in range(groups - 2):

            @pl.when(passes(slot))
            def _():
                pass_copy(buf, recv_sem, pass_sem, slot).wait_send()

    chain_copy(0).start()
    send_groups(st_src, st_buf, st_send, st_recv, lambda copy: copy.start())

    def send_chunk(chunk):

        @pl.when(has_two_ahead)
        def _():
            for part in (0, 1):
                ahead_two(part, chunk).start()

        @pl.when(is_even)
        def _():
            for part in (0, 1):
                ahead_one(part, chunk).start()

    for chunk in ORDER[:AHEAD]:
        send_chunk(chunk)

    @pl.when(me < 2)
    def _():
        keeps[0] = jnp.zeros((16, BLOCK), jnp.bfloat16)
        kcat[0:BLOCK, :] = jnp.zeros((BLOCK, WIDTH), jnp.bfloat16)
        vcat[0:BLOCK, :] = jnp.zeros((BLOCK, WIDTH), jnp.bfloat16)

    @pl.when(me < 1)
    def _():
        keeps[1] = jnp.zeros((16, BLOCK), jnp.bfloat16)
        kcat[BLOCK : 2 * BLOCK, :] = jnp.zeros((BLOCK, WIDTH), jnp.bfloat16)
        vcat[BLOCK : 2 * BLOCK, :] = jnp.zeros((BLOCK, WIDTH), jnp.bfloat16)

    for slot in range(groups - 1):

        @pl.when(slot >= window)
        def _():
            st_buf[slot] = jnp.zeros((FAR_ROWS, FAR_COLS), jnp.bfloat16)
            fx_buf[slot] = jnp.zeros((FAR_ROWS, FAR_COLS), jnp.bfloat16)

    @pl.when(has_two_back)
    def _():
        keep_copy(2).wait_recv()

    @pl.when(has_one_back)
    def _():
        keep_copy(1).wait_recv()

    def as_bias(flags):
        return jnp.where(flags > 0.5, 0.0, NEG)

    for slot in (0, 1):
        row = as_bias(keeps[slot][0:1, :].astype(jnp.float32))
        bias[:, slot * BLOCK : (slot + 1) * BLOCK] = jnp.broadcast_to(row, (BLOCK, BLOCK))
    query_ids = lax.broadcasted_iota(jnp.int32, (BLOCK, BLOCK), 0)
    key_ids = lax.broadcasted_iota(jnp.int32, (BLOCK, BLOCK), 1)
    flags = jnp.where(key_ids == query_ids, 1.0, jnp.broadcast_to(keep_row, (BLOCK, BLOCK)))
    bias[:, 2 * BLOCK :] = as_bias(jnp.where(key_ids <= query_ids, flags, 0.0))

    def attend(chunk, far):
        rows = []
        for buf, flag in far:
            keep = buf[BLOCK : BLOCK + 16, 0:BLOCK].astype(jnp.float32)[0:1, :]
            rows.append(as_bias(keep * flag))
        for h in range(CHUNK_HEADS):
            at = chunk * CHUNK + h * HEAD_DIM
            head = pl.ds(at, HEAD_DIM)
            far_head = (chunk * CHUNK_HEADS + h - LOCAL_HEADS) % FAR_HEADS
            far_at = far_head // HALF_HEADS * HALF + far_head % HALF_HEADS * HEAD_DIM
            q = q_ref[:, head]
            nt = (((1,), (1,)), ((), ()))
            near = lax.dot_general(q, kcat[:, head], nt, preferred_element_type=jnp.float32)
            scores = [near * SCALE + bias[...]]
            for (buf, _), row in zip(far, rows):
                keys = buf[0:BLOCK, far_at : far_at + HEAD_DIM]
                term = lax.dot_general(q, keys, nt, preferred_element_type=jnp.float32)
                scores.append(term * SCALE + row)
            top = jnp.max(scores[0], axis=1, keepdims=True)
            for s in scores[1:]:
                top = jnp.maximum(top, jnp.max(s, axis=1, keepdims=True))
            total = 0.0
            weighted = 0.0
            for i, s in enumerate(scores):
                w = jnp.exp2(s - top)
                total = total + jnp.sum(w, axis=1, keepdims=True)
                if i == 0:
                    values = vcat[:, head]
                else:
                    far_values = far_at + HALF_KEYS
                    values = far[i - 1][0][0:BLOCK, far_values : far_values + HEAD_DIM]
                weighted = weighted + jnp.dot(
                    w.astype(jnp.bfloat16), values, preferred_element_type=jnp.float32)
            o_ref[:, head] = (weighted / total).astype(jnp.bfloat16)

    def chain_step(step):
        chain_copy(step).wait_recv()
        if step == steps:
            send_groups(fin, fx_buf, fx_send, fx_recv, lambda copy: copy.start())
            return
        bit = 1 << step
        theirs = lax.rem(lax.div(pos_ref[window], bit), 2)
        mine = lax.rem(lax.div(column, bit), 2)
        take = jnp.abs(theirs - mine).astype(jnp.float32)
        held = fx_src[:, mine_half] if step == 0 else half[step - 1]
        kept = held.astype(jnp.float32) * (1.0 - take) + rcv[step].astype(jnp.float32) * take
        if step + 1 < steps:
            half[step] = kept.astype(jnp.bfloat16)
        else:
            fin[:, mine_half] = kept.astype(jnp.bfloat16)
        chain_copy(step + 1).start()

    def own_sent(chunk):

        @pl.when(has_two_ahead)
        def _():
            for part in (0, 1):
                ahead_two(part, chunk).wait_send()

        @pl.when(is_even)
        def _():
            for part in (0, 1):
                ahead_one(part, chunk).wait_send()

    loads[2].wait()
    spacing = 2 if 2 * steps + 1 < ORDER.index(FIXED_CHUNK) else 1
    for turn, chunk in enumerate(ORDER):
        if turn + AHEAD < CHUNKS:
            own_sent(chunk)
            send_chunk(ORDER[turn + AHEAD])

        @pl.when(has_two_back)
        def _():
            for part in (0, 1):
                ahead_two(part, chunk).wait_recv()

        @pl.when(forwards)
        def _():
            for part in (0, 1):
                forward(part, chunk).start()

        if turn == CHUNKS // 3:
            pass_groups(st_buf, st_recv, st_pass)
        if chunk == FIXED_CHUNK:
            pass_groups(fx_buf, fx_recv, fx_pass)

        @pl.when(has_one_back)
        def _():
            for part in (0, 1):
                ahead_one(part, chunk).wait_recv()

        far = []
        if chunk == STRIDED_CHUNK:
            rest_of_groups(st_buf, st_recv, st_pass)
        if chunk >= STRIDED_CHUNK:
            for slot in range(groups - 1):
                far.append((st_buf.at[slot], (slot < window).astype(jnp.float32)))
        if chunk == FIXED_CHUNK:
            rest_of_groups(fx_buf, fx_recv, fx_pass)
        if FIXED_CHUNK <= chunk < STRIDED_CHUNK:
            for slot in range(groups - 1):
                used = (slot < window) & (slot * stride + pos_ref[slot] < me - LOOKBACK)
                far.append((fx_buf.at[slot], used.astype(jnp.float32)))
            used = window * stride + pos_ref[window] < me - LOOKBACK
            far.append((fin, used.astype(jnp.float32)))
        if turn % spacing == 1 % spacing and turn // spacing <= steps:
            chain_step(turn // spacing)
        attend(chunk, far)

    @pl.when(has_one_ahead)
    def _():
        keep_copy(1).wait_send()

    @pl.when(has_two_ahead)
    def _():
        keep_copy(2).wait_send()

    for chunk in ORDER[CHUNKS - AHEAD :]:
        own_sent(chunk)

    @pl.when(forwards)
    def _():
        for chunk in ORDER:
            for part in (0, 1):
                forward(part, chunk).wait_send()

    for step in range(steps + 1):
        chain_copy(step).wait_send()
    send_groups(st_src, st_buf, st_send, st_recv, lambda copy: copy.wait_send())
    send_groups(fin, fx_buf, fx_send, fx_recv, lambda copy: copy.wait_send())
    passed_on(st_buf, st_recv, st_pass)
    passed_on(fx_buf, fx_recv, fx_pass)


def on_device(queries, key_states, value_states, key_keep, summary_pos, *, stride, groups):
    steps = stride.bit_length() - 1
    assert 1 << steps == stride and 1 < steps < FIXED_CHUNK and groups % 2 == 0
    vmem = pl.BlockSpec(memory_space=pltpu.VMEM)
    hbm = pl.BlockSpec(memory_space=pl.ANY)
    dma = pltpu.SemaphoreType.DMA
    far = (FAR_ROWS, FAR_COLS)
    return pl.pallas_call(
        functools.partial(kernel, stride, groups),
        out_shape=jax.ShapeDtypeStruct((BLOCK, WIDTH), jnp.bfloat16),
        in_specs=[pl.BlockSpec(memory_space=pltpu.SMEM), hbm, hbm, hbm, vmem],
        out_specs=vmem,
        scratch_shapes=[
            pltpu.VMEM((BLOCK, WIDTH), jnp.bfloat16),
            pltpu.VMEM((3 * BLOCK, WIDTH), jnp.bfloat16),
            pltpu.VMEM((3 * BLOCK, WIDTH), jnp.bfloat16),
            pltpu.VMEM((3, 16, BLOCK), jnp.bfloat16),
            pltpu.VMEM((BLOCK, 3 * BLOCK), jnp.float32),
            pltpu.VMEM(far, jnp.bfloat16),
            pltpu.VMEM((groups - 1,) + far, jnp.bfloat16),
            pltpu.VMEM(far, jnp.bfloat16),
            pltpu.VMEM((steps - 1, FAR_ROWS, HALF), jnp.bfloat16),
            pltpu.VMEM((steps, FAR_ROWS, HALF), jnp.bfloat16),
            pltpu.VMEM(far, jnp.bfloat16),
            pltpu.VMEM((groups - 1,) + far, jnp.bfloat16),
            dma((2, 2, CHUNKS)), dma((2, 2, CHUNKS)),
            dma((2,)), dma((2,)),
            dma((steps + 1,)), dma((steps + 1,)),
            dma((groups - 1,)), dma((groups - 1,)), dma((groups - 1,)),
            dma((groups - 1,)), dma((groups - 1,)), dma((groups - 1,)),
            dma((3,)),
        ],
        compiler_params=pltpu.CompilerParams(
            collective_id=0, has_side_effects=True, vmem_limit_bytes=40 * 1024 * 1024),
    )(summary_pos, queries, key_states, value_states, key_keep.reshape(1, BLOCK))


def solution(mesh):
    rows = P(("grp", "seq"), None)
    return jax.shard_map(
        functools.partial(on_device, stride=mesh.shape["seq"], groups=mesh.shape["grp"]),
        mesh=mesh,
        in_specs=(rows, rows, rows, P(("grp", "seq")), P()),
        out_specs=rows,
        check_vma=False,
    )
```

```python
import functools
import math

import jax
import jax.numpy as jnp
from jax import lax
from jax.experimental import pallas as pl
from jax.experimental.pallas import tpu as pltpu
from jax.sharding import PartitionSpec as P

HEADS = 24
HEAD_DIM = 128
FIXED_HEADS = 4
STRIDED_HEADS = 4
LOCAL_HEADS = 16
BLOCK = 128
LOOKBACK = 2
WIDTH = HEADS * HEAD_DIM

CHUNK_HEADS = 2
CHUNK = CHUNK_HEADS * HEAD_DIM
CHUNKS = HEADS // CHUNK_HEADS
FIXED_CHUNK = LOCAL_HEADS // CHUNK_HEADS
STRIDED_CHUNK = (LOCAL_HEADS + FIXED_HEADS) // CHUNK_HEADS
ORDER = tuple(range(FIXED_CHUNK)) + tuple(range(STRIDED_CHUNK, CHUNKS)) + tuple(range(FIXED_CHUNK, STRIDED_CHUNK))
FAR_HEADS = 4
FAR_ROWS = BLOCK + 16
FAR_COLS = 2 * FAR_HEADS * HEAD_DIM
HALF = FAR_COLS // 2
HALF_HEADS = FAR_HEADS // 2
HALF_KEYS = HALF_HEADS * HEAD_DIM

AHEAD = 4
NEG = -1e30
SCALE = math.log2(math.e) / math.sqrt(HEAD_DIM)
MESH = pl.DeviceIdType.MESH


def kernel(
    stride, groups, pos_ref, q_hbm, k_hbm, v_hbm, keep_ref, o_ref,
    q_ref, kcat, vcat, keeps, bias, st_src, st_buf, fx_src, half, rcv, fin, fx_buf,
    halo_send, halo_recv, keep_send, keep_recv, ch_send, ch_recv,
    st_send, st_recv, st_pass, fx_send, fx_recv, fx_pass, load_sem,
):
    steps = stride.bit_length() - 1
    blocks = stride * groups
    window = lax.axis_index("grp")
    column = lax.axis_index("seq")
    me = window * stride + column
    odd = lax.rem(column, 2)
    is_odd = odd == 1
    is_even = odd == 0
    core = lax.rem(window, 2)
    chip = window - core
    own_rows = pl.ds(LOOKBACK * BLOCK, BLOCK)
    loads = [
        pltpu.make_async_copy(src, dst, load_sem.at[i])
        for i, (src, dst) in enumerate(
            ((k_hbm, kcat.at[own_rows]), (v_hbm, vcat.at[own_rows]), (q_hbm, q_ref)))
    ]
    for load in loads:
        load.start()

    def device(block):
        return (lax.div(block, stride), lax.rem(block, stride))

    def partner(step):
        bit = 1 << step
        mine = lax.rem(lax.div(column, bit), 2)
        return (window, column + bit * (1 - 2 * mine))

    def cols(chunk):
        return pl.ds(chunk * CHUNK, CHUNK)

    barrier = pltpu.get_barrier_semaphore()
    greeted = 0
    for away in (-2, -1, 1, 2):
        there = (me + away >= 0) & (me + away < blocks)

        @pl.when(there)
        def _():
            pl.semaphore_signal(barrier, inc=1, device_id=device(me + away), device_id_type=MESH)

        greeted = greeted + there.astype(jnp.int32)
    for step in range(steps):
        pl.semaphore_signal(barrier, inc=1, device_id=partner(step), device_id_type=MESH)
    for away in range(1, groups):
        other = lax.rem(window + away, groups)
        pl.semaphore_signal(barrier, inc=1, device_id=(other, column), device_id_type=MESH)

    keep_row = keep_ref[...].astype(jnp.float32)
    keep_tile = jnp.broadcast_to(keep_row, (16, BLOCK)).astype(jnp.bfloat16)
    keeps[2] = keep_tile
    loads[0].wait()
    loads[1].wait()
    for buf, first in ((st_src, LOCAL_HEADS + FIXED_HEADS), (fx_src, LOCAL_HEADS)):
        for i in (0, 1):
            some = pl.ds(first * HEAD_DIM + i * HALF_KEYS, HALF_KEYS)
            buf[0:BLOCK, i * HALF : i * HALF + HALF_KEYS] = kcat[own_rows, some]
            buf[0:BLOCK, i * HALF + HALF_KEYS : (i + 1) * HALF] = vcat[own_rows, some]
        for lane in range(0, FAR_COLS, BLOCK):
            buf[BLOCK:FAR_ROWS, lane : lane + BLOCK] = keep_tile

    pl.semaphore_wait(barrier, greeted + (steps + groups - 1))

    def keep_copy(ahead):
        slot = LOOKBACK - ahead
        return pltpu.make_async_remote_copy(
            src_ref=keeps.at[2], dst_ref=keeps.at[slot],
            send_sem=keep_send.at[slot], recv_sem=keep_recv.at[slot],
            device_id=device(jnp.minimum(me + ahead, blocks - 1)), device_id_type=MESH)

    mine_half = pl.ds(pl.multiple_of(odd * HALF, HALF), HALF)
    other_half = pl.ds(pl.multiple_of((1 - odd) * HALF, HALF), HALF)

    def chain_copy(step):
        if step == 0:
            src, dst = fx_src.at[:, other_half], rcv.at[0]
        elif step < steps:
            src, dst = half.at[step - 1], rcv.at[step]
        else:
            src, dst = fin.at[:, mine_half], fin.at[:, mine_half]
        return pltpu.make_async_remote_copy(
            src_ref=src, dst_ref=dst,
            send_sem=ch_send.at[step], recv_sem=ch_recv.at[step],
            device_id=partner(step % steps), device_id_type=MESH)

    def group_copy(src, buf, send_sem, recv_sem, away):
        return pltpu.make_async_remote_copy(
            src_ref=src, dst_ref=buf.at[window],
            send_sem=send_sem.at[away - 1], recv_sem=recv_sem.at[window],
            device_id=(window + away, column), device_id_type=MESH)

    def halo_copy(slot, part, chunk, src, target):
        cat = (kcat, vcat)[part]
        return pltpu.make_async_remote_copy(
            src_ref=src, dst_ref=cat.at[pl.ds(slot * BLOCK, BLOCK), cols(chunk)],
            send_sem=halo_send.at[slot, part, chunk], recv_sem=halo_recv.at[slot, part, chunk],
            device_id=device(target), device_id_type=MESH)

    def own(part, chunk):
        return (kcat, vcat)[part].at[own_rows, cols(chunk)]

    def ahead_two(part, chunk):
        return halo_copy(0, part, chunk, own(part, chunk), me + 2)

    def ahead_one(part, chunk):
        return halo_copy(1, part, chunk, own(part, chunk), me + 1)

    def forward(part, chunk):
        src = (kcat, vcat)[part].at[pl.ds(0, BLOCK), cols(chunk)]
        return halo_copy(1, part, chunk, src, me - 1)

    has_two_ahead = me + 2 < blocks
    has_one_ahead = me + 1 < blocks
    has_two_back = me >= 2
    has_one_back = me >= 1
    forwards = is_odd & has_two_back

    @pl.when(has_one_ahead)
    def _():
        keep_copy(1).start()

    @pl.when(has_two_ahead)
    def _():
        keep_copy(2).start()

    def goes(away):
        if away == 1:
            return core == 0
        return (window + away < groups) & (away % 2 == 0)

    def send_groups(src, buf, send_sem, recv_sem, act):
        for away in range(1, groups):
            if away == 1 or away % 2 == 0:

                @pl.when(goes(away))
                def _():
                    act(group_copy(src, buf, send_sem, recv_sem, away))

    def pass_copy(buf, recv_sem, pass_sem, slot):
        return pltpu.make_async_remote_copy(
            src_ref=buf.at[slot], dst_ref=buf.at[slot],
            send_sem=pass_sem.at[slot], recv_sem=recv_sem.at[slot],
            device_id=(chip + 1 - core, column), device_id_type=MESH)

    def passes(slot):
        return (slot < chip) & (core == slot % 2)

    def pass_groups(buf, recv_sem, pass_sem):
        for slot in range(groups - 2):

            @pl.when(passes(slot))
            def _():
                copy = pass_copy(buf, recv_sem, pass_sem, slot)
                copy.wait_recv()
                copy.start()

    def rest_of_groups(buf, recv_sem, pass_sem):
        for slot in range(groups - 1):

            @pl.when((slot < window) & jnp.logical_not(passes(slot)))
            def _():
                pass_copy(buf, recv_sem, pass_sem, slot).wait_recv()

    def passed_on(buf, recv_sem, pass_sem):
        for slot in range(groups - 2):

            @pl.when(passes(slot))
            def _():
                pass_copy(buf, recv_sem, pass_sem, slot).wait_send()

    chain_copy(0).start()
    send_groups(st_src, st_buf, st_send, st_recv, lambda copy: copy.start())

    def send_chunk(chunk):

        @pl.when(has_two_ahead)
        def _():
            for part in (0, 1):
                ahead_two(part, chunk).start()

        @pl.when(is_even)
        def _():
            for part in (0, 1):
                ahead_one(part, chunk).start()

    for chunk in ORDER[:AHEAD]:
        send_chunk(chunk)

    @pl.when(me < 2)
    def _():
        keeps[0] = jnp.zeros((16, BLOCK), jnp.bfloat16)
        kcat[0:BLOCK, :] = jnp.zeros((BLOCK, WIDTH), jnp.bfloat16)
        vcat[0:BLOCK, :] = jnp.zeros((BLOCK, WIDTH), jnp.bfloat16)

    @pl.when(me < 1)
    def _():
        keeps[1] = jnp.zeros((16, BLOCK), jnp.bfloat16)
        kcat[BLOCK : 2 * BLOCK, :] = jnp.zeros((BLOCK, WIDTH), jnp.bfloat16)
        vcat[BLOCK : 2 * BLOCK, :] = jnp.zeros((BLOCK, WIDTH), jnp.bfloat16)

    for slot in range(groups - 1):

        @pl.when(slot >= window)
        def _():
            st_buf[slot] = jnp.zeros((FAR_ROWS, FAR_COLS), jnp.bfloat16)
            fx_buf[slot] = jnp.zeros((FAR_ROWS, FAR_COLS), jnp.bfloat16)

    @pl.when(has_two_back)
    def _():
        keep_copy(2).wait_recv()

    @pl.when(has_one_back)
    def _():
        keep_copy(1).wait_recv()

    def as_bias(flags):
        return jnp.where(flags > 0.5, 0.0, NEG)

    for slot in (0, 1):
        row = as_bias(keeps[slot][0:1, :].astype(jnp.float32))
        bias[:, slot * BLOCK : (slot + 1) * BLOCK] = jnp.broadcast_to(row, (BLOCK, BLOCK))
    query_ids = lax.broadcasted_iota(jnp.int32, (BLOCK, BLOCK), 0)
    key_ids = lax.broadcasted_iota(jnp.int32, (BLOCK, BLOCK), 1)
    flags = jnp.where(key_ids == query_ids, 1.0, jnp.broadcast_to(keep_row, (BLOCK, BLOCK)))
    bias[:, 2 * BLOCK :] = as_bias(jnp.where(key_ids <= query_ids, flags, 0.0))

    def attend(chunk, far):
        rows = []
        for buf, flag in far:
            keep = buf[BLOCK : BLOCK + 16, 0:BLOCK].astype(jnp.float32)[0:1, :]
            rows.append(as_bias(keep * flag))
        for h in range(CHUNK_HEADS):
            at = chunk * CHUNK + h * HEAD_DIM
            head = pl.ds(at, HEAD_DIM)
            far_head = (chunk * CHUNK_HEADS + h - LOCAL_HEADS) % FAR_HEADS
            far_at = far_head // HALF_HEADS * HALF + far_head % HALF_HEADS * HEAD_DIM
            q = q_ref[:, head]
            nt = (((1,), (1,)), ((), ()))
            near = lax.dot_general(q, kcat[:, head], nt, preferred_element_type=jnp.float32)
            scores = [near * SCALE + bias[...]]
            for (buf, _), row in zip(far, rows):
                keys = buf[0:BLOCK, far_at : far_at + HEAD_DIM]
                term = lax.dot_general(q, keys, nt, preferred_element_type=jnp.float32)
                scores.append(term * SCALE + row)
            top = jnp.max(scores[0], axis=1, keepdims=True)
            for s in scores[1:]:
                top = jnp.maximum(top, jnp.max(s, axis=1, keepdims=True))
            total = 0.0
            weighted = 0.0
            for i, s in enumerate(scores):
                w = jnp.exp2(s - top)
                total = total + jnp.sum(w, axis=1, keepdims=True)
                if i == 0:
                    values = vcat[:, head]
                else:
                    far_values = far_at + HALF_KEYS
                    values = far[i - 1][0][0:BLOCK, far_values : far_values + HEAD_DIM]
                weighted = weighted + jnp.dot(
                    w.astype(jnp.bfloat16), values, preferred_element_type=jnp.float32)
            o_ref[:, head] = (weighted / total).astype(jnp.bfloat16)

    def chain_step(step):
        chain_copy(step).wait_recv()
        if step == steps:
            send_groups(fin, fx_buf, fx_send, fx_recv, lambda copy: copy.start())
            return
        bit = 1 << step
        theirs = lax.rem(lax.div(pos_ref[window], bit), 2)
        mine = lax.rem(lax.div(column, bit), 2)
        take = jnp.abs(theirs - mine).astype(jnp.float32)
        held = fx_src[:, mine_half] if step == 0 else half[step - 1]
        kept = held.astype(jnp.float32) * (1.0 - take) + rcv[step].astype(jnp.float32) * take
        if step + 1 < steps:
            half[step] = kept.astype(jnp.bfloat16)
        else:
            fin[:, mine_half] = kept.astype(jnp.bfloat16)
        chain_copy(step + 1).start()

    def own_sent(chunk):

        @pl.when(has_two_ahead)
        def _():
            for part in (0, 1):
                ahead_two(part, chunk).wait_send()

        @pl.when(is_even)
        def _():
            for part in (0, 1):
                ahead_one(part, chunk).wait_send()

    loads[2].wait()
    spacing = 2 if 2 * steps + 1 < ORDER.index(FIXED_CHUNK) else 1
    for turn, chunk in enumerate(ORDER):
        if turn + AHEAD < CHUNKS:
            own_sent(chunk)
            send_chunk(ORDER[turn + AHEAD])

        @pl.when(has_two_back)
        def _():
            for part in (0, 1):
                ahead_two(part, chunk).wait_recv()

        @pl.when(forwards)
        def _():
            for part in (0, 1):
                forward(part, chunk).start()

        if turn == CHUNKS // 3:
            pass_groups(st_buf, st_recv, st_pass)
        if chunk == FIXED_CHUNK:
            pass_groups(fx_buf, fx_recv, fx_pass)

        @pl.when(has_one_back)
        def _():
            for part in (0, 1):
                ahead_one(part, chunk).wait_recv()

        far = []
        if chunk == STRIDED_CHUNK:
            rest_of_groups(st_buf, st_recv, st_pass)
        if chunk >= STRIDED_CHUNK:
            for slot in range(groups - 1):
                far.append((st_buf.at[slot], (slot < window).astype(jnp.float32)))
        if chunk == FIXED_CHUNK:
            rest_of_groups(fx_buf, fx_recv, fx_pass)
        if FIXED_CHUNK <= chunk < STRIDED_CHUNK:
            for slot in range(groups - 1):
                used = (slot < window) & (slot * stride + pos_ref[slot] < me - LOOKBACK)
                far.append((fx_buf.at[slot], used.astype(jnp.float32)))
            used = window * stride + pos_ref[window] < me - LOOKBACK
            far.append((fin, used.astype(jnp.float32)))
        if turn % spacing == 1 % spacing and turn // spacing <= steps:
            chain_step(turn // spacing)
        attend(chunk, far)

    @pl.when(has_one_ahead)
    def _():
        keep_copy(1).wait_send()

    @pl.when(has_two_ahead)
    def _():
        keep_copy(2).wait_send()

    for chunk in ORDER[CHUNKS - AHEAD :]:
        own_sent(chunk)

    @pl.when(forwards)
    def _():
        for chunk in ORDER:
            for part in (0, 1):
                forward(part, chunk).wait_send()

    for step in range(steps + 1):
        chain_copy(step).wait_send()
    send_groups(st_src, st_buf, st_send, st_recv, lambda copy: copy.wait_send())
    send_groups(fin, fx_buf, fx_send, fx_recv, lambda copy: copy.wait_send())
    passed_on(st_buf, st_recv, st_pass)
    passed_on(fx_buf, fx_recv, fx_pass)


def on_device(queries, key_states, value_states, key_keep, summary_pos, *, stride, groups):
    steps = stride.bit_length() - 1
    assert 1 << steps == stride and 1 < steps < FIXED_CHUNK and groups % 2 == 0
    vmem = pl.BlockSpec(memory_space=pltpu.VMEM)
    hbm = pl.BlockSpec(memory_space=pl.ANY)
    dma = pltpu.SemaphoreType.DMA
    far = (FAR_ROWS, FAR_COLS)
    return pl.pallas_call(
        functools.partial(kernel, stride, groups),
        out_shape=jax.ShapeDtypeStruct((BLOCK, WIDTH), jnp.bfloat16),
        in_specs=[pl.BlockSpec(memory_space=pltpu.SMEM), hbm, hbm, hbm, vmem],
        out_specs=vmem,
        scratch_shapes=[
            pltpu.VMEM((BLOCK, WIDTH), jnp.bfloat16),
            pltpu.VMEM((3 * BLOCK, WIDTH), jnp.bfloat16),
            pltpu.VMEM((3 * BLOCK, WIDTH), jnp.bfloat16),
            pltpu.VMEM((3, 16, BLOCK), jnp.bfloat16),
            pltpu.VMEM((BLOCK, 3 * BLOCK), jnp.float32),
            pltpu.VMEM(far, jnp.bfloat16),
            pltpu.VMEM((groups - 1,) + far, jnp.bfloat16),
            pltpu.VMEM(far, jnp.bfloat16),
            pltpu.VMEM((steps - 1, FAR_ROWS, HALF), jnp.bfloat16),
            pltpu.VMEM((steps, FAR_ROWS, HALF), jnp.bfloat16),
            pltpu.VMEM(far, jnp.bfloat16),
            pltpu.VMEM((groups - 1,) + far, jnp.bfloat16),
            dma((2, 2, CHUNKS)), dma((2, 2, CHUNKS)),
            dma((2,)), dma((2,)),
            dma((steps + 1,)), dma((steps + 1,)),
            dma((groups - 1,)), dma((groups - 1,)), dma((groups - 1,)),
            dma((groups - 1,)), dma((groups - 1,)), dma((groups - 1,)),
            dma((3,)),
        ],
        compiler_params=pltpu.CompilerParams(
            collective_id=0, has_side_effects=True, vmem_limit_bytes=40 * 1024 * 1024),
    )(summary_pos, queries, key_states, value_states, key_keep.reshape(1, BLOCK))


def solution(mesh):
    rows = P(("grp", "seq"), None)
    return jax.shard_map(
        functools.partial(on_device, stride=mesh.shape["seq"], groups=mesh.shape["grp"]),
        mesh=mesh,
        in_specs=(rows, rows, rows, P(("grp", "seq")), P()),
        out_specs=rows,
        check_vma=False,
    )
```

```python
import functools
import math

import jax
import jax.numpy as jnp
from jax import lax
from jax.experimental import pallas as pl
from jax.experimental.pallas import tpu as pltpu
from jax.sharding import PartitionSpec as P

HEADS = 24
HEAD_DIM = 128
FIXED_HEADS = 4
STRIDED_HEADS = 4
LOCAL_HEADS = 16
BLOCK = 128
LOOKBACK = 2
WIDTH = HEADS * HEAD_DIM

CHUNK_HEADS = 4
CHUNK = CHUNK_HEADS * HEAD_DIM
CHUNKS = HEADS // CHUNK_HEADS
FIXED_CHUNK = LOCAL_HEADS // CHUNK_HEADS
STRIDED_CHUNK = (LOCAL_HEADS + FIXED_HEADS) // CHUNK_HEADS
ORDER = tuple(range(FIXED_CHUNK)) + (STRIDED_CHUNK, FIXED_CHUNK)
FAR_ROWS = BLOCK + 16
FAR_COLS = 2 * CHUNK
HALF = FAR_COLS // 2
HALF_HEADS = CHUNK_HEADS // 2
HALF_KEYS = HALF_HEADS * HEAD_DIM

AHEAD = 2
NEG = -1e30
SCALE = math.log2(math.e) / math.sqrt(HEAD_DIM)
MESH = pl.DeviceIdType.MESH


def kernel(
    stride, groups, pos_ref, q_hbm, k_hbm, v_hbm, keep_ref, o_ref,
    q_ref, kcat, vcat, keeps, bias, st_src, st_buf, fx_src, half, rcv, fin, fx_buf,
    halo_send, halo_recv, keep_send, keep_recv, ch_send, ch_recv,
    st_send, st_recv, st_pass, fx_send, fx_recv, fx_pass, load_sem,
):
    steps = stride.bit_length() - 1
    blocks = stride * groups
    window = lax.axis_index("grp")
    column = lax.axis_index("seq")
    me = window * stride + column
    odd = lax.rem(column, 2)
    is_odd = odd == 1
    is_even = odd == 0
    core = lax.rem(window, 2)
    chip = window - core
    own_rows = pl.ds(LOOKBACK * BLOCK, BLOCK)
    loads = [
        pltpu.make_async_copy(src, dst, load_sem.at[i])
        for i, (src, dst) in enumerate(
            ((k_hbm, kcat.at[own_rows]), (v_hbm, vcat.at[own_rows]), (q_hbm, q_ref)))
    ]
    for load in loads:
        load.start()

    def device(block):
        return (lax.div(block, stride), lax.rem(block, stride))

    def partner(step):
        bit = 1 << step
        mine = lax.rem(lax.div(column, bit), 2)
        return (window, column + bit * (1 - 2 * mine))

    def cols(chunk):
        return pl.ds(chunk * CHUNK, CHUNK)

    barrier = pltpu.get_barrier_semaphore()
    greeted = 0
    for away in (-2, -1, 1, 2):
        there = (me + away >= 0) & (me + away < blocks)

        @pl.when(there)
        def _():
            pl.semaphore_signal(barrier, inc=1, device_id=device(me + away), device_id_type=MESH)

        greeted = greeted + there.astype(jnp.int32)
    for step in range(steps):
        pl.semaphore_signal(barrier, inc=1, device_id=partner(step), device_id_type=MESH)
    for away in range(1, groups):
        other = lax.rem(window + away, groups)
        pl.semaphore_signal(barrier, inc=1, device_id=(other, column), device_id_type=MESH)

    keep_row = keep_ref[...].astype(jnp.float32)
    keep_tile = jnp.broadcast_to(keep_row, (16, BLOCK)).astype(jnp.bfloat16)
    keeps[2] = keep_tile
    loads[0].wait()
    loads[1].wait()
    for buf, chunk in ((st_src, STRIDED_CHUNK), (fx_src, FIXED_CHUNK)):
        for i in (0, 1):
            some = pl.ds(chunk * CHUNK + i * HALF_KEYS, HALF_KEYS)
            buf[0:BLOCK, i * HALF : i * HALF + HALF_KEYS] = kcat[own_rows, some]
            buf[0:BLOCK, i * HALF + HALF_KEYS : (i + 1) * HALF] = vcat[own_rows, some]
        for lane in range(0, FAR_COLS, BLOCK):
            buf[BLOCK:FAR_ROWS, lane : lane + BLOCK] = keep_tile

    pl.semaphore_wait(barrier, greeted + (steps + groups - 1))

    def keep_copy(ahead):
        slot = LOOKBACK - ahead
        return pltpu.make_async_remote_copy(
            src_ref=keeps.at[2], dst_ref=keeps.at[slot],
            send_sem=keep_send.at[slot], recv_sem=keep_recv.at[slot],
            device_id=device(jnp.minimum(me + ahead, blocks - 1)), device_id_type=MESH)

    mine_half = pl.ds(pl.multiple_of(odd * HALF, HALF), HALF)
    other_half = pl.ds(pl.multiple_of((1 - odd) * HALF, HALF), HALF)

    def chain_copy(step):
        if step == 0:
            src, dst = fx_src.at[:, other_half], rcv.at[0]
        elif step < steps:
            src, dst = half.at[step - 1], rcv.at[step]
        else:
            src, dst = fin.at[:, mine_half], fin.at[:, mine_half]
        return pltpu.make_async_remote_copy(
            src_ref=src, dst_ref=dst,
            send_sem=ch_send.at[step], recv_sem=ch_recv.at[step],
            device_id=partner(step % steps), device_id_type=MESH)

    def group_copy(src, buf, send_sem, recv_sem, away):
        return pltpu.make_async_remote_copy(
            src_ref=src, dst_ref=buf.at[window],
            send_sem=send_sem.at[away - 1], recv_sem=recv_sem.at[window],
            device_id=(window + away, column), device_id_type=MESH)

    def halo_copy(slot, part, chunk, src, target):
        cat = (kcat, vcat)[part]
        return pltpu.make_async_remote_copy(
            src_ref=src, dst_ref=cat.at[pl.ds(slot * BLOCK, BLOCK), cols(chunk)],
            send_sem=halo_send.at[slot, part, chunk], recv_sem=halo_recv.at[slot, part, chunk],
            device_id=device(target), device_id_type=MESH)

    def own(part, chunk):
        return (kcat, vcat)[part].at[own_rows, cols(chunk)]

    def ahead_two(part, chunk):
        return halo_copy(0, part, chunk, own(part, chunk), me + 2)

    def ahead_one(part, chunk):
        return halo_copy(1, part, chunk, own(part, chunk), me + 1)

    def forward(part, chunk):
        src = (kcat, vcat)[part].at[pl.ds(0, BLOCK), cols(chunk)]
        return halo_copy(1, part, chunk, src, me - 1)

    has_two_ahead = me + 2 < blocks
    has_one_ahead = me + 1 < blocks
    has_two_back = me >= 2
    has_one_back = me >= 1
    forwards = is_odd & has_two_back

    @pl.when(has_one_ahead)
    def _():
        keep_copy(1).start()

    @pl.when(has_two_ahead)
    def _():
        keep_copy(2).start()

    def goes(away):
        if away == 1:
            return core == 0
        return (window + away < groups) & (away % 2 == 0)

    def send_groups(src, buf, send_sem, recv_sem, act):
        for away in range(1, groups):
            if away == 1 or away % 2 == 0:

                @pl.when(goes(away))
                def _():
                    act(group_copy(src, buf, send_sem, recv_sem, away))

    def pass_copy(buf, recv_sem, pass_sem, slot):
        return pltpu.make_async_remote_copy(
            src_ref=buf.at[slot], dst_ref=buf.at[slot],
            send_sem=pass_sem.at[slot], recv_sem=recv_sem.at[slot],
            device_id=(chip + 1 - core, column), device_id_type=MESH)

    def passes(slot):
        return (slot < chip) & (core == slot % 2)

    def pass_groups(buf, recv_sem, pass_sem):
        for slot in range(groups - 2):

            @pl.when(passes(slot))
            def _():
                copy = pass_copy(buf, recv_sem, pass_sem, slot)
                copy.wait_recv()
                copy.start()

    def rest_of_groups(buf, recv_sem, pass_sem):
        for slot in range(groups - 1):

            @pl.when((slot < window) & jnp.logical_not(passes(slot)))
            def _():
                pass_copy(buf, recv_sem, pass_sem, slot).wait_recv()

    def passed_on(buf, recv_sem, pass_sem):
        for slot in range(groups - 2):

            @pl.when(passes(slot))
            def _():
                pass_copy(buf, recv_sem, pass_sem, slot).wait_send()

    chain_copy(0).start()
    send_groups(st_src, st_buf, st_send, st_recv, lambda copy: copy.start())

    def send_chunk(chunk):

        @pl.when(has_two_ahead)
        def _():
            for part in (0, 1):
                ahead_two(part, chunk).start()

        @pl.when(is_even)
        def _():
            for part in (0, 1):
                ahead_one(part, chunk).start()

    for chunk in ORDER[:AHEAD]:
        send_chunk(chunk)

    @pl.when(me < 2)
    def _():
        keeps[0] = jnp.zeros((16, BLOCK), jnp.bfloat16)
        kcat[0:BLOCK, :] = jnp.zeros((BLOCK, WIDTH), jnp.bfloat16)
        vcat[0:BLOCK, :] = jnp.zeros((BLOCK, WIDTH), jnp.bfloat16)

    @pl.when(me < 1)
    def _():
        keeps[1] = jnp.zeros((16, BLOCK), jnp.bfloat16)
        kcat[BLOCK : 2 * BLOCK, :] = jnp.zeros((BLOCK, WIDTH), jnp.bfloat16)
        vcat[BLOCK : 2 * BLOCK, :] = jnp.zeros((BLOCK, WIDTH), jnp.bfloat16)

    for slot in range(groups - 1):

        @pl.when(slot >= window)
        def _():
            st_buf[slot] = jnp.zeros((FAR_ROWS, FAR_COLS), jnp.bfloat16)
            fx_buf[slot] = jnp.zeros((FAR_ROWS, FAR_COLS), jnp.bfloat16)

    @pl.when(has_two_back)
    def _():
        keep_copy(2).wait_recv()

    @pl.when(has_one_back)
    def _():
        keep_copy(1).wait_recv()

    def as_bias(flags):
        return jnp.where(flags > 0.5, 0.0, NEG)

    for slot in (0, 1):
        row = as_bias(keeps[slot][0:1, :].astype(jnp.float32))
        bias[:, slot * BLOCK : (slot + 1) * BLOCK] = jnp.broadcast_to(row, (BLOCK, BLOCK))
    query_ids = lax.broadcasted_iota(jnp.int32, (BLOCK, BLOCK), 0)
    key_ids = lax.broadcasted_iota(jnp.int32, (BLOCK, BLOCK), 1)
    flags = jnp.where(key_ids == query_ids, 1.0, jnp.broadcast_to(keep_row, (BLOCK, BLOCK)))
    bias[:, 2 * BLOCK :] = as_bias(jnp.where(key_ids <= query_ids, flags, 0.0))

    def attend(chunk, far):
        rows = []
        for buf, flag in far:
            keep = buf[BLOCK : BLOCK + 16, 0:BLOCK].astype(jnp.float32)[0:1, :]
            rows.append(as_bias(keep * flag))
        for h in range(CHUNK_HEADS):
            at = chunk * CHUNK + h * HEAD_DIM
            head = pl.ds(at, HEAD_DIM)
            far_at = h // HALF_HEADS * HALF + h % HALF_HEADS * HEAD_DIM
            q = q_ref[:, head]
            nt = (((1,), (1,)), ((), ()))
            near = lax.dot_general(q, kcat[:, head], nt, preferred_element_type=jnp.float32)
            scores = [near * SCALE + bias[...]]
            for (buf, _), row in zip(far, rows):
                keys = buf[0:BLOCK, far_at : far_at + HEAD_DIM]
                term = lax.dot_general(q, keys, nt, preferred_element_type=jnp.float32)
                scores.append(term * SCALE + row)
            top = jnp.max(scores[0], axis=1, keepdims=True)
            for s in scores[1:]:
                top = jnp.maximum(top, jnp.max(s, axis=1, keepdims=True))
            total = 0.0
            weighted = 0.0
            for i, s in enumerate(scores):
                w = jnp.exp2(s - top)
                total = total + jnp.sum(w, axis=1, keepdims=True)
                if i == 0:
                    values = vcat[:, head]
                else:
                    far_values = far_at + HALF_KEYS
                    values = far[i - 1][0][0:BLOCK, far_values : far_values + HEAD_DIM]
                weighted = weighted + jnp.dot(
                    w.astype(jnp.bfloat16), values, preferred_element_type=jnp.float32)
            o_ref[:, head] = (weighted / total).astype(jnp.bfloat16)

    def chain_step(step):
        chain_copy(step).wait_recv()
        if step == steps:
            send_groups(fin, fx_buf, fx_send, fx_recv, lambda copy: copy.start())
            return
        bit = 1 << step
        theirs = lax.rem(lax.div(pos_ref[window], bit), 2)
        mine = lax.rem(lax.div(column, bit), 2)
        take = jnp.abs(theirs - mine).astype(jnp.float32)
        held = fx_src[:, mine_half] if step == 0 else half[step - 1]
        kept = held.astype(jnp.float32) * (1.0 - take) + rcv[step].astype(jnp.float32) * take
        if step + 1 < steps:
            half[step] = kept.astype(jnp.bfloat16)
        else:
            fin[:, mine_half] = kept.astype(jnp.bfloat16)
        chain_copy(step + 1).start()

    crosses = column >= stride - LOOKBACK

    def own_sent(chunk):

        @pl.when(has_two_ahead & jnp.logical_not(crosses))
        def _():
            for part in (0, 1):
                ahead_two(part, chunk).wait_send()

        @pl.when(is_even)
        def _():
            for part in (0, 1):
                ahead_one(part, chunk).wait_send()

    loads[2].wait()
    for turn, chunk in enumerate(ORDER):
        if turn + AHEAD < CHUNKS:
            own_sent(chunk)
            send_chunk(ORDER[turn + AHEAD])

        @pl.when(has_two_back)
        def _():
            for part in (0, 1):
                ahead_two(part, chunk).wait_recv()

        @pl.when(forwards)
        def _():
            for part in (0, 1):
                forward(part, chunk).start()

        if steps == CHUNKS - 1 == turn:
            chain_step(turn)
        if turn == AHEAD:
            pass_groups(st_buf, st_recv, st_pass)
        if chunk == FIXED_CHUNK:
            pass_groups(fx_buf, fx_recv, fx_pass)

        @pl.when(has_one_back)
        def _():
            for part in (0, 1):
                ahead_one(part, chunk).wait_recv()

        far = []
        if chunk == STRIDED_CHUNK:
            rest_of_groups(st_buf, st_recv, st_pass)
            for slot in range(groups - 1):
                far.append((st_buf.at[slot], (slot < window).astype(jnp.float32)))
        if chunk == FIXED_CHUNK:
            rest_of_groups(fx_buf, fx_recv, fx_pass)
            for slot in range(groups - 1):
                used = (slot < window) & (slot * stride + pos_ref[slot] < me - LOOKBACK)
                far.append((fx_buf.at[slot], used.astype(jnp.float32)))
            used = window * stride + pos_ref[window] < me - LOOKBACK
            far.append((fin, used.astype(jnp.float32)))
        if turn <= steps and turn < CHUNKS - 1:
            chain_step(turn)
        attend(chunk, far)

    @pl.when(has_one_ahead)
    def _():
        keep_copy(1).wait_send()

    @pl.when(has_two_ahead)
    def _():
        keep_copy(2).wait_send()

    for chunk in ORDER[CHUNKS - AHEAD :]:
        own_sent(chunk)

    @pl.when(has_two_ahead & crosses)
    def _():
        for chunk in ORDER:
            for part in (0, 1):
                ahead_two(part, chunk).wait_send()

    @pl.when(forwards)
    def _():
        for chunk in ORDER:
            for part in (0, 1):
                forward(part, chunk).wait_send()

    for step in range(steps + 1):
        chain_copy(step).wait_send()
    send_groups(st_src, st_buf, st_send, st_recv, lambda copy: copy.wait_send())
    send_groups(fin, fx_buf, fx_send, fx_recv, lambda copy: copy.wait_send())
    passed_on(st_buf, st_recv, st_pass)
    passed_on(fx_buf, fx_recv, fx_pass)


def on_device(queries, key_states, value_states, key_keep, summary_pos, *, stride, groups):
    steps = stride.bit_length() - 1
    assert 1 << steps == stride and 1 < steps < CHUNKS and groups % 2 == 0
    vmem = pl.BlockSpec(memory_space=pltpu.VMEM)
    hbm = pl.BlockSpec(memory_space=pl.ANY)
    dma = pltpu.SemaphoreType.DMA
    far = (FAR_ROWS, FAR_COLS)
    return pl.pallas_call(
        functools.partial(kernel, stride, groups),
        out_shape=jax.ShapeDtypeStruct((BLOCK, WIDTH), jnp.bfloat16),
        in_specs=[pl.BlockSpec(memory_space=pltpu.SMEM), hbm, hbm, hbm, vmem],
        out_specs=vmem,
        scratch_shapes=[
            pltpu.VMEM((BLOCK, WIDTH), jnp.bfloat16),
            pltpu.VMEM((3 * BLOCK, WIDTH), jnp.bfloat16),
            pltpu.VMEM((3 * BLOCK, WIDTH), jnp.bfloat16),
            pltpu.VMEM((3, 16, BLOCK), jnp.bfloat16),
            pltpu.VMEM((BLOCK, 3 * BLOCK), jnp.float32),
            pltpu.VMEM(far, jnp.bfloat16),
            pltpu.VMEM((groups - 1,) + far, jnp.bfloat16),
            pltpu.VMEM(far, jnp.bfloat16),
            pltpu.VMEM((steps - 1, FAR_ROWS, HALF), jnp.bfloat16),
            pltpu.VMEM((steps, FAR_ROWS, HALF), jnp.bfloat16),
            pltpu.VMEM(far, jnp.bfloat16),
            pltpu.VMEM((groups - 1,) + far, jnp.bfloat16),
            dma((2, 2, CHUNKS)), dma((2, 2, CHUNKS)),
            dma((2,)), dma((2,)),
            dma((steps + 1,)), dma((steps + 1,)),
            dma((groups - 1,)), dma((groups - 1,)), dma((groups - 1,)),
            dma((groups - 1,)), dma((groups - 1,)), dma((groups - 1,)),
            dma((3,)),
        ],
        compiler_params=pltpu.CompilerParams(
            collective_id=0, has_side_effects=True, vmem_limit_bytes=40 * 1024 * 1024),
    )(summary_pos, queries, key_states, value_states, key_keep.reshape(1, BLOCK))


def solution(mesh):
    rows = P(("grp", "seq"), None)
    return jax.shard_map(
        functools.partial(on_device, stride=mesh.shape["seq"], groups=mesh.shape["grp"]),
        mesh=mesh,
        in_specs=(rows, rows, rows, P(("grp", "seq")), P()),
        out_specs=rows,
        check_vma=False,
    )
```
